32 devices in a mesh: section: 2 (over x), expert: 16 (over z, y, core).
Axes of the slice: x: 2, y: 2, z: 4, core: 2. Of those that a mesh axis runs over, the one named last changes fastest.
Arguments:
- emitted: bfloat16 [2, 2, 1024, 2048], P('section', None, 'expert'), may hold values from -6 to 6
- levels: int32 [2, 2, 1024], P('section', None, 'expert'), may hold values from 0 to 999
- expert_ids: int32 [2, 2, 1024, 6], P('section', None, 'expert'), may hold values from 0 to 15, all different within a row; in each aligned block of 64 rows (0 to 63, 64 to 127, ..., all dimensions but the last counted through in order) at most 32 rows name the same one
- gate_values: float32 [2, 2, 1024, 6], P('section', None, 'expert'), may hold values from 0.05 to 0.5
- w_gate: bfloat16 [2, 16, 2048, 768], P('section', 'expert'), may hold values from -0.125 to 0.125
- w_up: bfloat16 [2, 16, 2048, 768], P('section', 'expert'), may hold values from -0.125 to 0.125
- w_down: bfloat16 [2, 16, 768, 2048], P('section', 'expert'), may hold values from -0.21875 to 0.21875
- w_mod: bfloat16 [2, 256, 4096], P('section'), may hold values from -0.375 to 0.375
Outputs:
- layer_out: bfloat16 [2, 2, 1024, 2048], P('section', None, 'expert')
The draws below stay inside these ranges and needn't reach their ends.
Inputs may be any that keep to these rules, and one draw needn't show every extreme that they name: `expert_ids`: each token names 6 different experts. Among the 64 tokens of one device of expert in one microbatch at one section, no expert is named by more than 32 tokens, and in every draw some expert is named by exactly 32 of them.
All inputs are finite; a program needn't handle non-finite values.
Results may differ from the reference program's by a relative error of at most 0.006.
Values may be sent and summed in bfloat16 or wider, within the bound.
No kernel may reach another device: no remote copies, remote signals or barrier semaphores. Data moves between devices by JAX's collectives and lax.ppermute only.
A program may use at most 64 MiB of HBM per device.

```python
import math
import jax
import jax.numpy as jnp
import numpy as np
from jax import lax

D = 2048
FF = 768
TOP = 6
FREQ = 256
LEVELS = 1000
MB = 2
TOK_DEV = 64
SECTIONS = 2
EXPERTS = 16
CAP = 32
TOKENS = 1024
N_SECTION = 2
N_EXPERT = 16


def touch_ends(values, rng, smallest, top_value):
    longest = values.shape.index(max(values.shape))
    spots = []
    for shift in (0, 1):
        where = [jax.random.randint(jax.random.fold_in(rng, axis), (), 0, length) for axis, length in enumerate(values.shape)]
        where[longest] = (where[longest] + shift) % values.shape[longest]
        spots.append(tuple(where))
    return values.at[spots[0]].set(smallest).at[spots[1]].set(top_value)


def block_levels(own_key, extent, shards, low, top_value):
    factor_of = 1.0
    for dim, blocks in shards:
        draws = jax.random.uniform(jax.random.fold_in(jax.random.fold_in(own_key, 6), dim), (blocks,), jnp.float32, low / len(shards), top_value / len(shards))
        factor_of = factor_of * jnp.repeat(jnp.exp(draws), extent[dim] // blocks).reshape((-1,) + (1,) * (len(extent) - 1 - dim))
    return factor_of


def assign_block(rng, own, number, rows, number_of, top, most, slope):
    order = jax.random.permutation(rng, number_of)
    crowded, common = portions_of(number_of, rows * top, most, slope, True), portions_of(number_of, rows * top, most, slope, False)
    places = jnp.arange(number_of)

    def named(sizes, turn):
        used = int((sizes > 0).sum())
        fixed = max(1, used // 4)
        moved = fixed + (places - fixed + turn * (used - fixed)) % max(1, number_of - fixed)
        return jnp.zeros((number_of,), jnp.int32).at[order[jnp.where(places < fixed, places, moved)]].set(jnp.asarray(sizes, jnp.int32))

    sizes = jnp.where(number % 4 == 0, named(crowded, number // 4), named(common, number - number // 4 - 1))
    mixed = jax.random.permutation(jax.random.fold_in(own, 3), number_of)
    source_of, taker = mixed[0:number_of // 2 * 2:2], mixed[1:number_of // 2 * 2:2]
    room = jnp.minimum(sizes[source_of] - 1, most - sizes[taker]) // 2
    room = jnp.where((source_of == order[0]) | (taker == order[0]) | (sizes[taker] == 0), 0, jnp.maximum(room, 0))
    moved = jax.random.randint(jax.random.fold_in(own, 4), (number_of // 2,), 0, 1 << 20) % (room + 1)
    sizes = sizes.at[source_of].add(-moved).at[taker].add(moved)
    items = jnp.searchsorted(jnp.cumsum(sizes), jnp.arange(rows * top), side="right").astype(jnp.int32)
    grid = items.reshape(top, rows).T
    grid = grid[jax.random.permutation(jax.random.fold_in(own, 1), rows)]
    turn = jax.random.randint(jax.random.fold_in(own, 2), (rows, 1), 0, top)
    return jnp.take_along_axis(grid, (jnp.arange(top)[None, :] + turn) % top, axis=1)


def portions_of(amount, total, reach, lean, full):
    loads = [(1 << 20) // math.isqrt(standing ** lean) + 1 for standing in range(1, amount + 1)]
    largest = reach if full else min(reach, max(-(-total // amount), total * loads[0] // sum(loads)))
    least = 1 if total - largest >= amount - 1 else 0
    holding, spare = [largest] + [least] * (amount - 1), total - largest - least * (amount - 1)
    while spare > 0:
        free = [i for i in range(1, amount) if holding[i] < largest] or [i for i in range(1, amount) if holding[i] < reach]
        mass, remaining = sum([loads[i] for i in free]), spare
        for i in free:
            extra = min(reach - holding[i], max(1, remaining * loads[i] // mass), spare)
            holding[i] = holding[i] + extra
            spare = spare - extra
    return np.array(holding)


def noise(own_key, extent, deviation, most, pieces=(), held_as=jnp.bfloat16):
    drawn = deviation * jax.random.normal(own_key, extent, jnp.float32)
    if pieces:
        drawn = drawn * block_levels(own_key, extent, pieces, -0.22, 0.18)
    return jnp.clip(drawn, -most, most).astype(held_as)


def setup_inputs(seed: int = 0) -> dict:
    keys = jax.random.split(jax.random.key(seed), 9)
    emitted = noise(keys[0], (SECTIONS, MB, TOKENS, D), 1.0, 6.0, ((0, 2), (2, 16)))
    levels = touch_ends(jax.random.randint(keys[1], (SECTIONS, MB, TOKENS), 0, LEVELS), jax.random.fold_in(keys[1], 1), 0, LEVELS - 1).astype(jnp.int32)
    expert_ids_keys = jax.random.split(jax.random.fold_in(keys[2], 1), SECTIONS * MB * TOKENS // TOK_DEV)
    expert_ids_turns = jax.random.permutation(jax.random.fold_in(keys[2], 3), SECTIONS * MB * TOKENS // TOK_DEV)
    expert_ids = jax.vmap(lambda own, number: assign_block(jax.random.fold_in(keys[2], 2), own, number, TOK_DEV, EXPERTS, TOP, CAP, 2))(expert_ids_keys, expert_ids_turns).reshape((SECTIONS, MB, TOKENS, TOP))
    gate_values = jnp.clip(0.05 + 0.45 * jax.random.uniform(keys[3], (SECTIONS, MB, TOKENS, TOP), jnp.float32) ** block_levels(keys[3], (SECTIONS, MB, TOKENS, TOP), ((0, 2), (2, 16)), -0.2, 0.2), 0.05, 0.5)
    w_gate = noise(keys[4], (SECTIONS, EXPERTS, D, FF), D ** -0.5, 0.125, ((0, 2), (1, 16)))
    w_up = noise(keys[5], (SECTIONS, EXPERTS, D, FF), D ** -0.5, 0.125, ((0, 2), (1, 16)))
    w_down = noise(keys[6], (SECTIONS, EXPERTS, FF, D), FF ** -0.5, 0.21875, ((0, 2), (1, 16)))
    w_mod = noise(keys[7], (SECTIONS, FREQ, 2 * D), FREQ ** -0.5, 0.375, ((0, 2),))
    return dict(emitted=emitted, levels=levels, expert_ids=expert_ids, gate_values=gate_values, w_gate=w_gate, w_up=w_up, w_down=w_down, w_mod=w_mod)


epsilon = 1e-06

def level_embedding(levels, entries):
    half_width = entries // 2
    frequency = jnp.exp(-math.log(10000.0) * jnp.arange(half_width, dtype=jnp.float32) / half_width)
    angles = levels.astype(jnp.float32)[:, None] * frequency[None, :]
    return jnp.concatenate([jnp.cos(angles), jnp.sin(angles)], axis=1).astype(jnp.bfloat16)

def modulate(tokens_in, levels, mod_weight):
    features = tokens_in.shape[1]
    embed = level_embedding(levels, mod_weight.shape[0])
    modulation = jnp.dot(embed, mod_weight, preferred_element_type=jnp.float32)
    values = tokens_in.astype(jnp.float32)
    mean_square = lax.optimization_barrier(jnp.mean(values * values, axis=1, keepdims=True))
    normed = values * lax.rsqrt(mean_square + epsilon) * (1.0 + modulation[:, :features]) + modulation[:, features:]
    return normed.astype(jnp.bfloat16)

def slot_table(id_block, experts):
    flat_ids = id_block.reshape(-1).astype(jnp.int32)
    onehot = (flat_ids[:, None] == jnp.arange(experts, dtype=jnp.int32)[None, :]).astype(jnp.int32)
    before = jnp.cumsum(onehot, axis=0) - onehot
    slot_pos = lax.optimization_barrier(jnp.sum(before * onehot, axis=1)).astype(jnp.int32)
    return (flat_ids, slot_pos)

def fill_buffer(normed, flat_ids, slot_pos, experts, capacity):
    chosen = flat_ids.shape[0] // normed.shape[0]
    token_index = (jnp.arange(flat_ids.shape[0], dtype=jnp.int32) // chosen).astype(jnp.int32)
    placing = (flat_ids * capacity + slot_pos).astype(jnp.int32)
    buffer = jnp.zeros((experts * capacity, normed.shape[1]), normed.dtype)
    buffer = buffer.at[placing].set(normed[token_index])
    return (buffer.reshape(experts, capacity, normed.shape[1]), placing)

def expert_rows(received, gate_weight, up_weight, down_weight):
    sources, per_source, features = received.shape
    row_data = received.reshape(sources * per_source, features)
    gate_part = jnp.dot(row_data, gate_weight, preferred_element_type=jnp.float32)
    up_part = jnp.dot(row_data, up_weight, preferred_element_type=jnp.float32)
    hidden = (jax.nn.silu(gate_part) * up_part).astype(jnp.bfloat16)
    produced = jnp.dot(hidden, down_weight, preferred_element_type=jnp.float32).astype(jnp.bfloat16)
    return produced.reshape(sources, per_source, features)

def combine(tokens_in, returned, placing, gate_block):
    count_rows, chosen = gate_block.shape
    features = tokens_in.shape[1]
    picked = returned.reshape(-1, features)[placing].astype(jnp.float32).reshape(count_rows, chosen, features)
    combined = tokens_in.astype(jnp.float32) + lax.optimization_barrier(jnp.sum(gate_block[:, :, None].astype(jnp.float32) * picked, axis=1))
    return combined.astype(jnp.bfloat16)

def run_expert(packed):
    return expert_rows(packed[0], packed[1], packed[2], packed[3])

def reference(emitted, levels, expert_ids, gate_values, w_gate, w_up, w_down, w_mod):
    arrived = jnp.roll(emitted, 1, axis=0)

    def build_block(normed_block, id_block):
        flat_ids, slot_pos = slot_table(id_block, EXPERTS)
        return fill_buffer(normed_block, flat_ids, slot_pos, EXPERTS, CAP)
    section_outs = []
    for section_index in range(N_SECTION):
        batch_outs = []
        for batch_index in range(MB):
            tokens_in = arrived[section_index, batch_index]
            normed = modulate(tokens_in, levels[section_index, batch_index], w_mod[section_index])
            normed_blocks = normed.reshape(N_EXPERT, TOK_DEV, D)
            id_blocks = expert_ids[section_index, batch_index].reshape(N_EXPERT, TOK_DEV, TOP)
            buffers, placings = jax.vmap(build_block)(normed_blocks, id_blocks)
            by_expert = jnp.swapaxes(buffers, 0, 1)
            produced = lax.map(run_expert, (by_expert, w_gate[section_index], w_up[section_index], w_down[section_index]))
            returned = jnp.swapaxes(produced, 0, 1)
            gate_blocks = gate_values[section_index, batch_index].reshape(N_EXPERT, TOK_DEV, TOP)
            token_blocks = tokens_in.reshape(N_EXPERT, TOK_DEV, D)
            outs = jax.vmap(combine)(token_blocks, returned, placings, gate_blocks)
            batch_outs.append(outs.reshape(TOKENS, D))
        section_outs.append(jnp.stack(batch_outs))
    return jnp.stack(section_outs)
```

```python
import math

import jax
import jax.numpy as jnp
from jax import lax
from jax.sharding import PartitionSpec as P

epsilon = 1e-06
CORES = 2
LANES = 128


def level_embedding(levels, entries):
    half_width = entries // 2
    frequency = jnp.exp(-math.log(10000.0) * jnp.arange(half_width, dtype=jnp.float32) / half_width)
    angles = levels.astype(jnp.float32)[:, None] * frequency[None, :]
    return jnp.concatenate([jnp.cos(angles), jnp.sin(angles)], axis=1).astype(jnp.bfloat16)


def chip_cycle(mesh):
    line = list(mesh.devices.reshape(mesh.devices.shape[0], -1)[0])
    chips = len(line) // CORES
    places = [tuple(getattr(line[CORES * c], "coords", (0, 0, c))) for c in range(chips)]
    spans = [sorted({p[d] for p in places}) for d in range(3)]
    wide = [d for d in range(3) if len(spans[d]) > 1]
    if len(set(places)) != chips or len(wide) != 2 or math.prod(len(spans[d]) for d in wide) != chips:
        return list(range(chips))
    rows, cols = wide if len(spans[wide[0]]) % 2 == 0 else wide[::-1]
    if len(spans[rows]) % 2:
        return list(range(chips))
    if len(spans[rows]) > len(spans[cols]) and len(spans[cols]) % 2 == 0:
        rows, cols = cols, rows
    at = {(p[rows], p[cols]): c for c, p in enumerate(places)}
    order = []
    for i, r in enumerate(spans[rows]):
        along = spans[cols][1:]
        order += [(r, c) for c in (along if i % 2 == 0 else along[::-1])]
    order += [(r, spans[cols][0]) for r in reversed(spans[rows])]
    return [at[place] for place in order]


def build(cycle):
    chips = len(cycle)
    experts = chips * CORES
    far = chips // 2
    halved = chips % 2 == 0

    def hop(value, step):
        pairs = [
            (cycle[i] * CORES + c, cycle[(i + step) % chips] * CORES + c)
            for i in range(chips)
            for c in range(CORES)
        ]
        return lax.ppermute(value, "expert", pairs)

    def swap(value):
        return lax.ppermute(value, "expert", [(i, i ^ 1) for i in range(experts)])

    def shards(emitted, levels, expert_ids, gate_values, w_gate, w_up, w_down, w_mod):
        sections = lax.axis_size("section")
        batches, tok_rows, features = emitted.shape[1:]
        around = [(s, (s + 1) % sections) for s in range(sections)]
        arrived = [lax.ppermute(emitted[0, b], "section", around) for b in range(batches)]
        mine = (w_gate[0, 0], w_up[0, 0], w_down[0, 0])
        other = tuple(swap(w) for w in mine)
        me = lax.axis_index("expert")
        mod_weight = w_mod[0]

        def payload(b):
            embed = level_embedding(levels[0, b], mod_weight.shape[0])
            modulation = jnp.dot(embed, mod_weight, preferred_element_type=jnp.float32)
            values = arrived[b].astype(jnp.float32)
            mean_square = jnp.mean(values * values, axis=1, keepdims=True)
            normed = (
                values * lax.rsqrt(mean_square + epsilon) * (1.0 + modulation[:, :features])
                + modulation[:, features:]
            ).astype(jnp.bfloat16)
            gates = gate_values[0, b]
            high = lax.reduce_precision(gates, 8, 7)
            extra = jnp.concatenate(
                [
                    expert_ids[0, b].astype(jnp.bfloat16),
                    high.astype(jnp.bfloat16),
                    (gates - high).astype(jnp.bfloat16),
                ],
                axis=1,
            )
            lanes = -(-extra.shape[1] // LANES) * LANES
            extra = jnp.pad(extra, ((0, 0), (0, lanes - extra.shape[1])))
            return jnp.concatenate([normed, extra], axis=1)

        top = expert_ids.shape[3]

        def partial(block):
            normed = block[:, :features]
            extra = block[:, features : features + 3 * top].astype(jnp.float32)
            ids, gates = extra[:, :top], extra[:, top : 2 * top] + extra[:, 2 * top :]
            total = 0.0
            for (gate_weight, up_weight, down_weight), expert in ((mine, me), (other, me ^ 1)):
                weight = jnp.sum(
                    jnp.where(ids == expert.astype(jnp.float32), gates, 0.0), axis=1, keepdims=True
                )
                gate_part = jnp.dot(normed, gate_weight, preferred_element_type=jnp.float32)
                up_part = jnp.dot(normed, up_weight, preferred_element_type=jnp.float32)
                hidden = (jax.nn.silu(gate_part) * up_part * weight).astype(jnp.bfloat16)
                total += jnp.dot(hidden, down_weight, preferred_element_type=jnp.float32)
            return total.astype(jnp.bfloat16)

        def added(a, b):
            return (a.astype(jnp.float32) + b.astype(jnp.float32)).astype(jnp.bfloat16)

        results = []
        for b in range(batches):
            own = payload(b)
            forth, back = [own], [own]
            for k in range(1, far + 1):
                last = halved and k == far
                half = tok_rows // 2
                forth.append(hop(forth[-1][:half] if last else forth[-1], 1))
                back.append(hop(back[-1][half:] if last else back[-1], -1))
            near = jnp.concatenate(forth[:far] + back[1:far])
            away = jnp.concatenate([forth[far], back[far]])
            near_sum, away_sum = partial(near), partial(away)
            pieces = [near_sum[i * tok_rows : (i + 1) * tok_rows] for i in range(2 * far - 1)]
            forth_sum, back_sum = pieces[:far], [pieces[0]] + pieces[far:]
            fs, bs = away_sum[: away_sum.shape[0] // 2], away_sum[away_sum.shape[0] // 2 :]
            for k in range(far - 1, -1, -1):
                fs, bs = hop(fs, -1), hop(bs, 1)
                if k:
                    if halved and k == far - 1:
                        half = tok_rows // 2
                        fs = jnp.concatenate([added(fs, forth_sum[k][:half]), forth_sum[k][half:]])
                        bs = jnp.concatenate([back_sum[k][:half], added(bs, back_sum[k][half:])])
                    else:
                        fs, bs = added(fs, forth_sum[k]), added(bs, back_sum[k])
            total = (
                arrived[b].astype(jnp.float32)
                + pieces[0].astype(jnp.float32)
                + fs.astype(jnp.float32)
                + bs.astype(jnp.float32)
            )
            results.append(total.astype(jnp.bfloat16))
        return jnp.stack(results)[None]

    return shards


def solution(mesh):
    placed = (
        P("section", None, "expert", None),
        P("section", None, "expert"),
        P("section", None, "expert", None),
        P("section", None, "expert", None),
        P("section", "expert", None, None),
        P("section", "expert", None, None),
        P("section", "expert", None, None),
        P("section", None, None),
    )
    return jax.shard_map(
        build(chip_cycle(mesh)),
        mesh=mesh,
        in_specs=placed,
        out_specs=P("section", None, "expert", None),
        check_vma=False,
    )
```

```python
import functools
import math

import jax
import jax.numpy as jnp
from jax import lax
from jax.experimental import pallas as pl
from jax.experimental.pallas import tpu as pltpu
from jax.sharding import PartitionSpec as P

epsilon = 1e-06
CORES = 2
LANES = 128
FF_CHUNK = 256
OUT_CHUNK = 512
VMEM_GRANT = 16 << 20


def level_embedding(levels, entries):
    half_width = entries // 2
    frequency = jnp.exp(-math.log(10000.0) * jnp.arange(half_width, dtype=jnp.float32) / half_width)
    angles = levels.astype(jnp.float32)[:, None] * frequency[None, :]
    return jnp.concatenate([jnp.cos(angles), jnp.sin(angles)], axis=1).astype(jnp.bfloat16)


def chip_cycle(mesh):
    line = list(mesh.devices.reshape(mesh.devices.shape[0], -1)[0])
    chips = len(line) // CORES
    places = [tuple(getattr(line[CORES * c], "coords", (0, 0, c))) for c in range(chips)]
    spans = [sorted({p[d] for p in places}) for d in range(3)]
    wide = [d for d in range(3) if len(spans[d]) > 1]
    if len(set(places)) != chips or len(wide) != 2 or math.prod(len(spans[d]) for d in wide) != chips:
        return list(range(chips))
    rows, cols = wide if len(spans[wide[0]]) % 2 == 0 else wide[::-1]
    if len(spans[rows]) % 2:
        return list(range(chips))
    if len(spans[rows]) > len(spans[cols]) and len(spans[cols]) % 2 == 0:
        rows, cols = cols, rows
    at = {(p[rows], p[cols]): c for c, p in enumerate(places)}
    order = []
    for i, r in enumerate(spans[rows]):
        along = spans[cols][1:]
        order += [(r, c) for c in (along if i % 2 == 0 else along[::-1])]
    order += [(r, spans[cols][0]) for r in reversed(spans[rows])]
    return [at[place] for place in order]


def chunk_of(extent, most):
    return next(c for c in range(min(extent, most), 0, -1) if extent % c == 0)


def group_kernel(sizes, features, experts, ff, me_ref, *refs):
    count = len(sizes)
    blocks, weights = refs[:count], refs[count : count + 6]
    outs = refs[count + 6 : 2 * count + 6]
    rows, hidden = refs[2 * count + 6 :]
    ff_chunk, out_chunk = chunk_of(ff, FF_CHUNK), chunk_of(features, OUT_CHUNK)
    shares = [[], []]
    start = 0
    for block, size in zip(blocks, sizes):
        rows[start : start + size, :] = block[:, :features]
        extra = block[:, features:].astype(jnp.float32)
        lane = lax.broadcasted_iota(jnp.int32, extra.shape, 1)
        for i in range(CORES):
            expert = me_ref[0] ^ i
            named = (lane == expert) | (lane == expert + experts)
            shares[i].append(jnp.sum(jnp.where(named, extra, 0.0), axis=1, keepdims=True))
        start += size
    for i in range(CORES):
        share = jnp.concatenate(shares[i], axis=0)
        gate_weight, up_weight = weights[3 * i], weights[3 * i + 1]
        for c in range(0, ff, ff_chunk):
            part = slice(c, c + ff_chunk)
            gate = jnp.dot(rows[...], gate_weight[:, part], preferred_element_type=jnp.float32)
            up = jnp.dot(rows[...], up_weight[:, part], preferred_element_type=jnp.float32)
            value = gate / (1.0 + jnp.exp(-gate)) * up * share
            hidden[:, i * ff + c : i * ff + c + ff_chunk] = value.astype(jnp.bfloat16)
    for n in range(0, features, out_chunk):
        part = slice(n, n + out_chunk)
        total = jnp.dot(hidden[:, :ff], weights[2][:, part], preferred_element_type=jnp.float32)
        total += jnp.dot(hidden[:, ff:], weights[5][:, part], preferred_element_type=jnp.float32)
        total = total.astype(jnp.bfloat16)
        start = 0
        for out, size in zip(outs, sizes):
            out[:, part] = total[start : start + size]
            start += size


def load_kernel(*refs):
    count = len(refs) // 2
    sems = refs[2 * count]
    copies = [pltpu.make_async_copy(refs[i], refs[count + i], sems.at[i]) for i in range(count)]
    for copy in copies:
        copy.start()
    for copy in copies:
        copy.wait()


def in_vmem(values):
    return pl.pallas_call(
        load_kernel,
        out_shape=[pltpu.VMEM(value.shape, value.dtype) for value in values],
        in_specs=[pl.BlockSpec(memory_space=pltpu.HBM)] * len(values),
        out_specs=[pl.BlockSpec(memory_space=pltpu.VMEM)] * len(values),
        scratch_shapes=[pltpu.SemaphoreType.DMA((len(values),))],
        compiler_params=pltpu.CompilerParams(vmem_limit_bytes=1 << 20),
        cost_estimate=pl.CostEstimate(
            flops=0, bytes_accessed=2 * sum(v.size * v.dtype.itemsize for v in values), transcendentals=0
        ),
    )(*[pltpu.with_memory_space_constraint(value, pltpu.HBM) for value in values])


def group_sums(me, blocks, weights, experts):
    sizes = [block.shape[0] for block in blocks]
    total = sum(sizes)
    features, ff = weights[0].shape
    near = pl.BlockSpec(memory_space=pltpu.VMEM)
    operands = [pltpu.with_memory_space_constraint(a, pltpu.VMEM) for a in (*blocks, *weights)]
    return pl.pallas_call(
        functools.partial(group_kernel, sizes, features, experts, ff),
        out_shape=[pltpu.VMEM((size, features), jnp.bfloat16) for size in sizes],
        in_specs=[pl.BlockSpec(memory_space=pltpu.SMEM)] + [near] * len(operands),
        out_specs=[near] * len(sizes),
        scratch_shapes=[
            pltpu.VMEM((total, features), jnp.bfloat16),
            pltpu.VMEM((total, CORES * ff), jnp.bfloat16),
        ],
        compiler_params=pltpu.CompilerParams(vmem_limit_bytes=VMEM_GRANT),
        cost_estimate=pl.CostEstimate(
            flops=6 * CORES * total * features * ff,
            bytes_accessed=4 * total * features,
            transcendentals=CORES * total * ff,
        ),
    )(me, *operands)


def build(cycle):
    chips = len(cycle)
    experts = chips * CORES
    far = chips // 2
    halved = chips % 2 == 0

    def hop(value, step):
        pairs = [
            (cycle[i] * CORES + c, cycle[(i + step) % chips] * CORES + c)
            for i in range(chips)
            for c in range(CORES)
        ]
        return lax.ppermute(value, "expert", pairs)

    def swap(value):
        return lax.ppermute(value, "expert", [(i, i ^ 1) for i in range(experts)])

    def shards(emitted, levels, expert_ids, gate_values, w_gate, w_up, w_down, w_mod):
        sections = lax.axis_size("section")
        batches, tok_rows, features = emitted.shape[1:]
        half = tok_rows // 2
        around = [(s, (s + 1) % sections) for s in range(sections)]
        arrived = [lax.ppermute(emitted[0, b], "section", around) for b in range(batches)]
        mine = (w_gate[0, 0], w_up[0, 0], w_down[0, 0])
        weights = mine + tuple(swap(w) for w in mine)
        me = lax.axis_index("expert").astype(jnp.int32).reshape(1)
        mod_weight = w_mod[0]
        lanes = -(-2 * experts // LANES) * LANES

        def payload(b):
            embed = level_embedding(levels[0, b], mod_weight.shape[0])
            modulation = jnp.dot(embed, mod_weight, preferred_element_type=jnp.float32)
            values = arrived[b].astype(jnp.float32)
            mean_square = jnp.mean(values * values, axis=1, keepdims=True)
            normed = (
                values * lax.rsqrt(mean_square + epsilon) * (1.0 + modulation[:, :features])
                + modulation[:, features:]
            ).astype(jnp.bfloat16)
            named = expert_ids[0, b][:, :, None] == jnp.arange(experts, dtype=jnp.int32)
            shares = jnp.sum(jnp.where(named, gate_values[0, b][:, :, None], 0.0), axis=1)
            high = lax.reduce_precision(shares, 8, 7)
            extra = jnp.concatenate([high, shares - high], axis=1).astype(jnp.bfloat16)
            extra = jnp.pad(extra, ((0, 0), (0, lanes - extra.shape[1])))
            return jnp.concatenate([normed, extra], axis=1)

        def added(a, b):
            return (a.astype(jnp.float32) + b.astype(jnp.float32)).astype(jnp.bfloat16)

        def tied(values):
            return lax.optimization_barrier(values)

        chains = [(b, step) for b in range(batches) for step in (1, -1)]
        first_half = (batches + 1) // 2
        top = {
            (b, step): far if not halved or (step == 1) == (b < first_half) else far - 1 for b, step in chains
        }
        own = [payload(b) for b in range(batches)]
        blocks = {(*chain, 0): own[chain[0]] for chain in chains}
        sums = {}

        def add_sums(keys):
            for key, value in zip(keys, group_sums(me, [blocks[key] for key in keys], weights, experts)):
                sums[key] = value

        for k in range(1, far + 1):
            moving = [chain for chain in chains if top[chain] >= k]
            sent = [blocks[(*chain, k - 1)] for chain in moving]
            if k > 1:
                sent = tied(sent)
            got = [hop(value, chain[1]) for value, chain in zip(sent, moving)]
            keys = [(*chain, k - 1) for chain in chains]
            if k == 1:
                weights = in_vmem(weights)
                got, weights = tied((got, weights))
            elif k == 2:
                keys = [(b, 1, 0) for b in range(batches)] + [(*chain, 1) for chain in chains]
                add_sums(keys)
                got, done = tied((got, [sums[key] for key in keys]))
                sums.update(zip(keys, done))
            else:
                add_sums(keys)
                got, done = tied((got, [sums[key] for key in keys]))
                sums.update(zip(keys, done))
            blocks.update({(*chain, k): value for chain, value in zip(moving, got)})

        last_keys = [(*chain, far) for chain in chains if top[chain] == far]
        add_sums(last_keys)
        total = {}
        for chain in chains:
            value = sums[(*chain, top[chain])]
            for place in range(top[chain] - 1, -1, -1):
                value = hop(value, -chain[1])
                if place:
                    value = added(value, sums[(*chain, place)])
            total[chain] = value
        results = []
        for b in range(batches):
            value = arrived[b].astype(jnp.float32) + sums[(b, 1, 0)].astype(jnp.float32)
            for step in (1, -1):
                value += total[b, step].astype(jnp.float32)
            results.append(value.astype(jnp.bfloat16))
        return jnp.stack(results)[None]

    return shards


def solution(mesh):
    placed = (
        P("section", None, "expert", None),
        P("section", None, "expert"),
        P("section", None, "expert", None),
        P("section", None, "expert", None),
        P("section", "expert", None, None),
        P("section", "expert", None, None),
        P("section", "expert", None, None),
        P("section", None, None),
    )
    return jax.shard_map(
        build(chip_cycle(mesh)),
        mesh=mesh,
        in_specs=placed,
        out_specs=P("section", None, "expert", None),
        check_vma=False,
    )
```

```python
import functools
import math

import jax
import jax.numpy as jnp
from jax import lax
from jax.experimental import pallas as pl
from jax.experimental.pallas import tpu as pltpu
from jax.sharding import PartitionSpec as P

epsilon = 1e-06
CORES = 2
LANES = 128
FF_CHUNK = 256
OUT_CHUNK = 512
CHUNK_BLOCKS = 4
VMEM_GRANT = 16 << 20


def level_embedding(levels, entries):
    half_width = entries // 2
    frequency = jnp.exp(-math.log(10000.0) * jnp.arange(half_width, dtype=jnp.float32) / half_width)
    angles = levels.astype(jnp.float32)[:, None] * frequency[None, :]
    return jnp.concatenate([jnp.cos(angles), jnp.sin(angles)], axis=1).astype(jnp.bfloat16)


def chip_cycle(mesh):
    line = list(mesh.devices.reshape(mesh.devices.shape[0], -1)[0])
    chips = len(line) // CORES
    places = [tuple(getattr(line[CORES * c], "coords", (0, 0, c))) for c in range(chips)]
    spans = [sorted({p[d] for p in places}) for d in range(3)]
    wide = [d for d in range(3) if len(spans[d]) > 1]
    if len(set(places)) != chips or len(wide) != 2 or math.prod(len(spans[d]) for d in wide) != chips:
        return list(range(chips))
    rows, cols = wide if len(spans[wide[0]]) % 2 == 0 else wide[::-1]
    if len(spans[rows]) % 2:
        return list(range(chips))
    if len(spans[rows]) > len(spans[cols]) and len(spans[cols]) % 2 == 0:
        rows, cols = cols, rows
    at = {(p[rows], p[cols]): c for c, p in enumerate(places)}
    order = []
    for i, r in enumerate(spans[rows]):
        along = spans[cols][1:]
        order += [(r, c) for c in (along if i % 2 == 0 else along[::-1])]
    order += [(r, spans[cols][0]) for r in reversed(spans[rows])]
    return [at[place] for place in order]


def chunk_of(extent, most):
    return next(c for c in range(min(extent, most), 0, -1) if extent % c == 0)


def dense_kernel(sizes, features, experts, ff, me_ref, *refs):
    count = len(sizes)
    blocks, weights = refs[:count], refs[count : count + 6]
    outs = refs[count + 6 : 2 * count + 6]
    rows, hidden = refs[2 * count + 6 :]
    ff_chunk, out_chunk = chunk_of(ff, FF_CHUNK), chunk_of(features, OUT_CHUNK)
    shares = [[], []]
    start = 0
    for block, size in zip(blocks, sizes):
        rows[start : start + size, :] = block[:, :features]
        extra = block[:, features:].astype(jnp.float32)
        lane = lax.broadcasted_iota(jnp.int32, extra.shape, 1)
        for i in range(CORES):
            expert = me_ref[0] ^ i
            named = (lane == expert) | (lane == expert + experts)
            shares[i].append(jnp.sum(jnp.where(named, extra, 0.0), axis=1, keepdims=True))
        start += size
    for i in range(CORES):
        share = jnp.concatenate(shares[i], axis=0)
        gate_weight, up_weight = weights[3 * i], weights[3 * i + 1]
        for c in range(0, ff, ff_chunk):
            part = slice(c, c + ff_chunk)
            gate = jnp.dot(rows[...], gate_weight[:, part], preferred_element_type=jnp.float32)
            up = jnp.dot(rows[...], up_weight[:, part], preferred_element_type=jnp.float32)
            value = gate / (1.0 + jnp.exp(-gate)) * up * share
            hidden[:, i * ff + c : i * ff + c + ff_chunk] = value.astype(jnp.bfloat16)
    for n in range(0, features, out_chunk):
        part = slice(n, n + out_chunk)
        total = jnp.dot(hidden[:, :ff], weights[2][:, part], preferred_element_type=jnp.float32)
        total += jnp.dot(hidden[:, ff:], weights[5][:, part], preferred_element_type=jnp.float32)
        total = total.astype(jnp.bfloat16)
        start = 0
        for out, size in zip(outs, sizes):
            out[:, part] = total[start : start + size]
            start += size


def picked_kernel(chunks, size, room, experts, me_ref, *refs):
    count = sum(chunks)
    blocks, weights = refs[:count], refs[count : count + 6]
    outs = refs[count + 6 : 2 * count + 6]
    picked, hidden, place = refs[2 * count + 6 :]
    features, ff = weights[0].shape
    ff_chunk, out_chunk = chunk_of(ff, FF_CHUNK), chunk_of(features, OUT_CHUNK)
    total = count * room
    shares = [[] for _ in range(CORES)]
    first = 0
    for chunk in chunks:
        tokens, slots = chunk * size, chunk * room
        values = jnp.concatenate([block[...] for block in blocks[first : first + chunk]], axis=0)
        extra = values[:, features:].astype(jnp.float32)
        lane = lax.broadcasted_iota(jnp.int32, extra.shape, 1)
        named = jnp.where(extra > 0.0, 1.0, 0.0)
        row = lax.broadcasted_iota(jnp.int32, (tokens, tokens), 0)
        column = lax.broadcasted_iota(jnp.int32, (tokens, tokens), 1)
        earlier = jnp.where((column < row) & (column // size == row // size), 1.0, 0.0)
        before = jnp.dot(
            earlier.astype(jnp.bfloat16), named.astype(jnp.bfloat16), preferred_element_type=jnp.float32
        )
        slot = lax.broadcasted_iota(jnp.int32, (tokens, slots), 1)
        start = lax.broadcasted_iota(jnp.int32, (tokens, slots), 0) // size * room
        for i in range(CORES):
            expert = me_ref[0] ^ i
            here = jnp.sum(jnp.where(lane == expert, before, 0.0), axis=1, keepdims=True)
            takes = jnp.sum(jnp.where(lane == expert, named, 0.0), axis=1, keepdims=True)
            match = (slot - start).astype(jnp.float32) == jnp.where(takes > 0.0, here, -1.0 * size * count)
            match = jnp.where(match, 1.0, 0.0).astype(jnp.bfloat16)
            place[first * size : first * size + tokens, i * slots : (i + 1) * slots] = match
            found = lax.dot_general(
                match, values, (((0,), (0,)), ((), ())), preferred_element_type=jnp.float32
            )
            at = i * total + first * room
            picked[at : at + slots, :] = found[:, :features].astype(jnp.bfloat16)
            both = lax.broadcasted_iota(jnp.int32, (slots, extra.shape[1]), 1)
            both = (both == expert) | (both == expert + experts)
            shares[i].append(jnp.sum(jnp.where(both, found[:, features:], 0.0), axis=1, keepdims=True))
        first += chunk
    for i in range(CORES):
        share = jnp.concatenate(shares[i], axis=0)
        gate_weight, up_weight = weights[3 * i], weights[3 * i + 1]
        rows = slice(i * total, (i + 1) * total)
        for c in range(0, ff, ff_chunk):
            part = slice(c, c + ff_chunk)
            gate = jnp.dot(picked[rows, :], gate_weight[:, part], preferred_element_type=jnp.float32)
            up = jnp.dot(picked[rows, :], up_weight[:, part], preferred_element_type=jnp.float32)
            value = gate / (1.0 + jnp.exp(-gate)) * up * share
            hidden[rows, part] = value.astype(jnp.bfloat16)
    for n in range(0, features, out_chunk):
        part = slice(n, n + out_chunk)
        made = [
            jnp.dot(
                hidden[i * total : (i + 1) * total, :],
                weights[3 * i + 2][:, part],
                preferred_element_type=jnp.float32,
            ).astype(jnp.bfloat16)
            for i in range(CORES)
        ]
        first = 0
        for chunk in chunks:
            tokens, slots = chunk * size, chunk * room
            mixed = jnp.concatenate([m[first * room : first * room + slots] for m in made], axis=0)
            spread = jnp.dot(
                place[first * size : first * size + tokens, : CORES * slots],
                mixed,
                preferred_element_type=jnp.float32,
            ).astype(jnp.bfloat16)
            for j in range(chunk):
                outs[first + j][:, part] = spread[j * size : (j + 1) * size]
            first += chunk


def load_kernel(*refs):
    count = len(refs) // 2
    sems = refs[2 * count]
    copies = [pltpu.make_async_copy(refs[i], refs[count + i], sems.at[i]) for i in range(count)]
    for copy in copies:
        copy.start()
    for copy in copies:
        copy.wait()


def in_vmem(values):
    return pl.pallas_call(
        load_kernel,
        out_shape=[pltpu.VMEM(value.shape, value.dtype) for value in values],
        in_specs=[pl.BlockSpec(memory_space=pltpu.HBM)] * len(values),
        out_specs=[pl.BlockSpec(memory_space=pltpu.VMEM)] * len(values),
        scratch_shapes=[pltpu.SemaphoreType.DMA((len(values),))],
        compiler_params=pltpu.CompilerParams(vmem_limit_bytes=1 << 20),
        cost_estimate=pl.CostEstimate(
            flops=0, bytes_accessed=0, transcendentals=0
        ),
    )(*[pltpu.with_memory_space_constraint(value, pltpu.HBM) for value in values])


def group_sums(me, blocks, weights, experts, room):
    count, size = len(blocks), blocks[0].shape[0]
    features, ff = weights[0].shape
    total = count * size
    if count >= CHUNK_BLOCKS:
        rows = count * room
        chunks = [min(CHUNK_BLOCKS, count - first) for first in range(0, count, CHUNK_BLOCKS)]
        kernel = functools.partial(picked_kernel, chunks, size, room, experts)
        scratch_shapes = [
            pltpu.VMEM((CORES * rows, features), jnp.bfloat16),
            pltpu.VMEM((CORES * rows, ff), jnp.bfloat16),
            pltpu.VMEM((total, CORES * CHUNK_BLOCKS * room), jnp.bfloat16),
        ]
    else:
        rows = total
        kernel = functools.partial(dense_kernel, [size] * count, features, experts, ff)
        scratch_shapes = [
            pltpu.VMEM((total, features), jnp.bfloat16),
            pltpu.VMEM((total, CORES * ff), jnp.bfloat16),
        ]
    near = pl.BlockSpec(memory_space=pltpu.VMEM)
    operands = [pltpu.with_memory_space_constraint(a, pltpu.VMEM) for a in (*blocks, *weights)]
    return pl.pallas_call(
        kernel,
        out_shape=[pltpu.VMEM((size, features), jnp.bfloat16)] * count,
        in_specs=[pl.BlockSpec(memory_space=pltpu.SMEM)] + [near] * len(operands),
        out_specs=[near] * count,
        scratch_shapes=scratch_shapes,
        compiler_params=pltpu.CompilerParams(vmem_limit_bytes=VMEM_GRANT),
        cost_estimate=pl.CostEstimate(
            flops=6 * CORES * rows * features * ff,
            bytes_accessed=4 * total * features,
            transcendentals=CORES * rows * ff,
        ),
    )(me, *operands)


def build(cycle):
    chips = len(cycle)
    experts = chips * CORES
    far = chips // 2
    halved = chips % 2 == 0

    def hop(value, step):
        pairs = [
            (cycle[i] * CORES + c, cycle[(i + step) % chips] * CORES + c)
            for i in range(chips)
            for c in range(CORES)
        ]
        return lax.ppermute(value, "expert", pairs)

    def swap(value):
        return lax.ppermute(value, "expert", [(i, i ^ 1) for i in range(experts)])

    def shards(emitted, levels, expert_ids, gate_values, w_gate, w_up, w_down, w_mod):
        sections = lax.axis_size("section")
        batches, tok_rows, features = emitted.shape[1:]
        half = tok_rows // 2
        around = [(s, (s + 1) % sections) for s in range(sections)]
        arrived = [lax.ppermute(emitted[0, b], "section", around) for b in range(batches)]
        mine = (w_gate[0, 0], w_up[0, 0], w_down[0, 0])
        down, arrived[0] = lax.optimization_barrier((mine[2], arrived[0]))
        weights = mine + (swap(mine[0]), swap(mine[1]), swap(down))
        room = min(tok_rows, 4 * tok_rows * expert_ids.shape[3] // (3 * experts))
        me = lax.axis_index("expert").astype(jnp.int32).reshape(1)
        mod_weight = w_mod[0]
        lanes = -(-2 * experts // LANES) * LANES

        def payload(b):
            embed = level_embedding(levels[0, b], mod_weight.shape[0])
            modulation = jnp.dot(embed, mod_weight, preferred_element_type=jnp.float32)
            values = arrived[b].astype(jnp.float32)
            mean_square = jnp.mean(values * values, axis=1, keepdims=True)
            normed = (
                values * lax.rsqrt(mean_square + epsilon) * (1.0 + modulation[:, :features])
                + modulation[:, features:]
            ).astype(jnp.bfloat16)
            named = expert_ids[0, b][:, :, None] == jnp.arange(experts, dtype=jnp.int32)
            shares = jnp.sum(jnp.where(named, gate_values[0, b][:, :, None], 0.0), axis=1)
            high = lax.reduce_precision(shares, 8, 7)
            extra = jnp.concatenate([high, shares - high], axis=1).astype(jnp.bfloat16)
            extra = jnp.pad(extra, ((0, 0), (0, lanes - extra.shape[1])))
            return jnp.concatenate([normed, extra], axis=1)

        def added(a, b):
            return (a.astype(jnp.float32) + b.astype(jnp.float32)).astype(jnp.bfloat16)

        def tied(values):
            return lax.optimization_barrier(values)

        chains = [(b, step) for b in range(batches) for step in (1, -1)]
        first_half = (batches + 1) // 2
        top = {
            (b, step): far if not halved or (step == 1) == (b < first_half) else far - 1 for b, step in chains
        }
        part = tok_rows // 2 if halved else tok_rows
        kept = {1: slice(0, part), -1: slice(tok_rows - part, tok_rows)}
        own = [payload(b) for b in range(batches)]
        blocks = {(*chain, 0): own[chain[0]] for chain in chains}
        sums = {}

        def add_sums(keys):
            for key, value in zip(keys, group_sums(me, [blocks[key] for key in keys], weights, experts, room)):
                sums[key] = value

        waiting = []
        for k in range(1, far + 1):
            for b in range(batches):
                moving = [(b, step) for step in (1, -1) if top[b, step] >= k]
                sent = [blocks[(*chain, k - 1)] for chain in moving]
                if waiting and b == batches - 1:
                    sent, done = tied((sent, [sums[key] for key in waiting]))
                    sums.update(zip(waiting, done))
                    waiting = []
                blocks.update({(*chain, k): hop(value, chain[1]) for value, chain in zip(sent, moving)})
            if k == 1:
                first = [(*chain, 1) for chain in chains]
                got, weights = tied(([blocks[key] for key in first], in_vmem(weights)))
                blocks.update(zip(first, got))
            else:
                waiting = [(*c, k - 1) for c in chains if k < far or top[c] == far]
                waiting += [(b, 1, 0) for b in range(batches)] if k == 2 else []
                add_sums(waiting)

        add_sums([(*chain, top[chain]) for chain in chains])
        total = {}
        for chain in chains:
            step = chain[1]
            if not halved:
                value = sums[(*chain, far)]
            else:
                value = next(sums[chain[0], way, far] for way in (1, -1) if top[chain[0], way] == far)[kept[step]]
            for place in range(far - 1, -1, -1):
                value = hop(value, -step)
                near = sums[(*chain, place)] if place else None
                if place and halved and place == far - 1:
                    fresh = added(value, near[kept[step]])
                    value = jnp.concatenate(
                        [fresh, near[part:]] if step == 1 else [near[: tok_rows - part], fresh]
                    )
                elif place:
                    value = added(value, near)
            total[chain] = value
        results = []
        for b in range(batches):
            value = arrived[b].astype(jnp.float32) + sums[(b, 1, 0)].astype(jnp.float32)
            for step in (1, -1):
                value += total[b, step].astype(jnp.float32)
            results.append(value.astype(jnp.bfloat16))
        return jnp.stack(results)[None]

    return shards


def solution(mesh):
    placed = (
        P("section", None, "expert", None),
        P("section", None, "expert"),
        P("section", None, "expert", None),
        P("section", None, "expert", None),
        P("section", "expert", None, None),
        P("section", "expert", None, None),
        P("section", "expert", None, None),
        P("section", None, None),
    )
    return jax.shard_map(
        build(chip_cycle(mesh)),
        mesh=mesh,
        in_specs=placed,
        out_specs=P("section", None, "expert", None),
        check_vma=False,
    )
```

```python
import functools
import math

import jax
import jax.numpy as jnp
from jax import lax
from jax.experimental import pallas as pl
from jax.experimental.pallas import tpu as pltpu
from jax.sharding import PartitionSpec as P

epsilon = 1e-06
CORES = 2
LANES = 128
FF_CHUNK = 256
OUT_CHUNK = 512
CHUNK_BLOCKS = 4
VMEM_GRANT = 16 << 20


def level_embedding(levels, entries):
    half_width = entries // 2
    frequency = jnp.exp(-math.log(10000.0) * jnp.arange(half_width, dtype=jnp.float32) / half_width)
    angles = levels.astype(jnp.float32)[:, None] * frequency[None, :]
    return jnp.concatenate([jnp.cos(angles), jnp.sin(angles)], axis=1).astype(jnp.bfloat16)


def chip_cycle(mesh):
    line = list(mesh.devices.reshape(mesh.devices.shape[0], -1)[0])
    chips = len(line) // CORES
    places = [tuple(getattr(line[CORES * c], "coords", (0, 0, c))) for c in range(chips)]
    spans = [sorted({p[d] for p in places}) for d in range(3)]
    wide = [d for d in range(3) if len(spans[d]) > 1]
    if len(set(places)) != chips or len(wide) != 2 or math.prod(len(spans[d]) for d in wide) != chips:
        return list(range(chips))
    rows, cols = wide if len(spans[wide[0]]) % 2 == 0 else wide[::-1]
    if len(spans[rows]) % 2:
        return list(range(chips))
    if len(spans[rows]) > len(spans[cols]) and len(spans[cols]) % 2 == 0:
        rows, cols = cols, rows
    at = {(p[rows], p[cols]): c for c, p in enumerate(places)}
    order = []
    for i, r in enumerate(spans[rows]):
        along = spans[cols][1:]
        order += [(r, c) for c in (along if i % 2 == 0 else along[::-1])]
    order += [(r, spans[cols][0]) for r in reversed(spans[rows])]
    return [at[place] for place in order]


def chunk_of(extent, most):
    return next(c for c in range(min(extent, most), 0, -1) if extent % c == 0)


def dense_kernel(sizes, features, experts, ff, me_ref, *refs):
    count = len(sizes)
    blocks, weights = refs[:count], refs[count : count + 6]
    outs = refs[count + 6 : 2 * count + 6]
    rows, hidden = refs[2 * count + 6 :]
    ff_chunk, out_chunk = chunk_of(ff, FF_CHUNK), chunk_of(features, OUT_CHUNK)
    shares = [[], []]
    start = 0
    for block, size in zip(blocks, sizes):
        rows[start : start + size, :] = block[:, :features]
        extra = block[:, features:].astype(jnp.float32)
        lane = lax.broadcasted_iota(jnp.int32, extra.shape, 1)
        for i in range(CORES):
            expert = me_ref[0] ^ i
            named = (lane == expert) | (lane == expert + experts)
            shares[i].append(jnp.sum(jnp.where(named, extra, 0.0), axis=1, keepdims=True))
        start += size
    for i in range(CORES):
        share = jnp.concatenate(shares[i], axis=0)
        gate_weight, up_weight = weights[3 * i], weights[3 * i + 1]
        for c in range(0, ff, ff_chunk):
            part = slice(c, c + ff_chunk)
            gate = jnp.dot(rows[...], gate_weight[:, part], preferred_element_type=jnp.float32)
            up = jnp.dot(rows[...], up_weight[:, part], preferred_element_type=jnp.float32)
            value = gate / (1.0 + jnp.exp(-gate)) * up * share
            hidden[:, i * ff + c : i * ff + c + ff_chunk] = value.astype(jnp.bfloat16)
    for n in range(0, features, out_chunk):
        part = slice(n, n + out_chunk)
        total = jnp.dot(hidden[:, :ff], weights[2][:, part], preferred_element_type=jnp.float32)
        total += jnp.dot(hidden[:, ff:], weights[5][:, part], preferred_element_type=jnp.float32)
        total = total.astype(jnp.bfloat16)
        start = 0
        for out, size in zip(outs, sizes):
            out[:, part] = total[start : start + size]
            start += size


def picked_kernel(chunks, size, room, experts, me_ref, *refs):
    count = sum(chunks)
    blocks, weights = refs[:count], refs[count : count + 6]
    outs = refs[count + 6 : 2 * count + 6]
    picked, hidden, place = refs[2 * count + 6 :]
    features, ff = weights[0].shape
    ff_chunk, out_chunk = chunk_of(ff, FF_CHUNK), chunk_of(features, OUT_CHUNK)
    total = count * room
    shares = [[] for _ in range(CORES)]
    first = 0
    for chunk in chunks:
        tokens, slots = chunk * size, chunk * room
        values = jnp.concatenate([block[...] for block in blocks[first : first + chunk]], axis=0)
        extra = values[:, features:].astype(jnp.float32)
        lane = lax.broadcasted_iota(jnp.int32, extra.shape, 1)
        named = jnp.where(extra > 0.0, 1.0, 0.0)
        row = lax.broadcasted_iota(jnp.int32, (tokens, tokens), 0)
        column = lax.broadcasted_iota(jnp.int32, (tokens, tokens), 1)
        earlier = jnp.where((column < row) & (column // size == row // size), 1.0, 0.0)
        before = jnp.dot(
            earlier.astype(jnp.bfloat16), named.astype(jnp.bfloat16), preferred_element_type=jnp.float32
        )
        slot = lax.broadcasted_iota(jnp.int32, (tokens, slots), 1)
        start = lax.broadcasted_iota(jnp.int32, (tokens, slots), 0) // size * room
        for i in range(CORES):
            expert = me_ref[0] ^ i
            here = jnp.sum(jnp.where(lane == expert, before, 0.0), axis=1, keepdims=True)
            takes = jnp.sum(jnp.where(lane == expert, named, 0.0), axis=1, keepdims=True)
            match = (slot - start).astype(jnp.float32) == jnp.where(takes > 0.0, here, -1.0 * size * count)
            match = jnp.where(match, 1.0, 0.0).astype(jnp.bfloat16)
            place[first * size : first * size + tokens, i * slots : (i + 1) * slots] = match
            found = lax.dot_general(
                match, values, (((0,), (0,)), ((), ())), preferred_element_type=jnp.float32
            )
            at = i * total + first * room
            picked[at : at + slots, :] = found[:, :features].astype(jnp.bfloat16)
            both = lax.broadcasted_iota(jnp.int32, (slots, extra.shape[1]), 1)
            both = (both == expert) | (both == expert + experts)
            shares[i].append(jnp.sum(jnp.where(both, found[:, features:], 0.0), axis=1, keepdims=True))
        first += chunk
    for i in range(CORES):
        share = jnp.concatenate(shares[i], axis=0)
        gate_weight, up_weight = weights[3 * i], weights[3 * i + 1]
        rows = slice(i * total, (i + 1) * total)
        for c in range(0, ff, ff_chunk):
            part = slice(c, c + ff_chunk)
            gate = jnp.dot(picked[rows, :], gate_weight[:, part], preferred_element_type=jnp.float32)
            up = jnp.dot(picked[rows, :], up_weight[:, part], preferred_element_type=jnp.float32)
            value = gate / (1.0 + jnp.exp(-gate)) * up * share
            hidden[rows, part] = value.astype(jnp.bfloat16)
    for n in range(0, features, out_chunk):
        part = slice(n, n + out_chunk)
        made = [
            jnp.dot(
                hidden[i * total : (i + 1) * total, :],
                weights[3 * i + 2][:, part],
                preferred_element_type=jnp.float32,
            ).astype(jnp.bfloat16)
            for i in range(CORES)
        ]
        first = 0
        for chunk in chunks:
            tokens, slots = chunk * size, chunk * room
            mixed = jnp.concatenate([m[first * room : first * room + slots] for m in made], axis=0)
            spread = jnp.dot(
                place[first * size : first * size + tokens, : CORES * slots],
                mixed,
                preferred_element_type=jnp.float32,
            ).astype(jnp.bfloat16)
            for j in range(chunk):
                outs[first + j][:, part] = spread[j * size : (j + 1) * size]
            first += chunk


def load_kernel(*refs):
    count = len(refs) // 2
    sems = refs[2 * count]
    copies = [pltpu.make_async_copy(refs[i], refs[count + i], sems.at[i]) for i in range(count)]
    for copy in copies:
        copy.start()
    for copy in copies:
        copy.wait()


def in_vmem(values):
    return pl.pallas_call(
        load_kernel,
        out_shape=[pltpu.VMEM(value.shape, value.dtype) for value in values],
        in_specs=[pl.BlockSpec(memory_space=pltpu.HBM)] * len(values),
        out_specs=[pl.BlockSpec(memory_space=pltpu.VMEM)] * len(values),
        scratch_shapes=[pltpu.SemaphoreType.DMA((len(values),))],
        compiler_params=pltpu.CompilerParams(vmem_limit_bytes=1 << 20),
        cost_estimate=pl.CostEstimate(
            flops=0, bytes_accessed=0, transcendentals=0
        ),
    )(*[pltpu.with_memory_space_constraint(value, pltpu.HBM) for value in values])


def group_sums(me, blocks, weights, experts, room):
    count, size = len(blocks), blocks[0].shape[0]
    features, ff = weights[0].shape
    total = count * size
    if count >= CHUNK_BLOCKS:
        rows = count * room
        chunks = [min(CHUNK_BLOCKS, count - first) for first in range(0, count, CHUNK_BLOCKS)]
        kernel = functools.partial(picked_kernel, chunks, size, room, experts)
        scratch_shapes = [
            pltpu.VMEM((CORES * rows, features), jnp.bfloat16),
            pltpu.VMEM((CORES * rows, ff), jnp.bfloat16),
            pltpu.VMEM((total, CORES * CHUNK_BLOCKS * room), jnp.bfloat16),
        ]
    else:
        rows = total
        kernel = functools.partial(dense_kernel, [size] * count, features, experts, ff)
        scratch_shapes = [
            pltpu.VMEM((total, features), jnp.bfloat16),
            pltpu.VMEM((total, CORES * ff), jnp.bfloat16),
        ]
    near = pl.BlockSpec(memory_space=pltpu.VMEM)
    operands = [pltpu.with_memory_space_constraint(a, pltpu.VMEM) for a in (*blocks, *weights)]
    return pl.pallas_call(
        kernel,
        out_shape=[pltpu.VMEM((size, features), jnp.bfloat16)] * count,
        in_specs=[pl.BlockSpec(memory_space=pltpu.SMEM)] + [near] * len(operands),
        out_specs=[near] * count,
        scratch_shapes=scratch_shapes,
        compiler_params=pltpu.CompilerParams(vmem_limit_bytes=VMEM_GRANT),
        cost_estimate=pl.CostEstimate(
            flops=6 * CORES * rows * features * ff,
            bytes_accessed=4 * total * features,
            transcendentals=CORES * rows * ff,
        ),
    )(me, *operands)


def build(cycle):
    chips = len(cycle)
    experts = chips * CORES
    far = chips // 2
    halved = chips % 2 == 0

    def hop(value, step):
        pairs = [
            (cycle[i] * CORES + c, cycle[(i + step) % chips] * CORES + c)
            for i in range(chips)
            for c in range(CORES)
        ]
        return lax.ppermute(value, "expert", pairs)

    def swap(value):
        return lax.ppermute(value, "expert", [(i, i ^ 1) for i in range(experts)])

    def shards(emitted, levels, expert_ids, gate_values, w_gate, w_up, w_down, w_mod):
        sections = lax.axis_size("section")
        batches, tok_rows, features = emitted.shape[1:]
        half = tok_rows // 2
        around = [(s, (s + 1) % sections) for s in range(sections)]
        arrived = [lax.ppermute(emitted[0, b], "section", around) for b in range(batches)]
        mine = (w_gate[0, 0], w_up[0, 0], w_down[0, 0])
        gate_other, down_other = swap(mine[0]), swap(mine[2])
        up_mine, gate_other = lax.optimization_barrier((mine[1], gate_other))
        weights = (*mine, gate_other, swap(up_mine), down_other)
        room = min(tok_rows, 4 * tok_rows * expert_ids.shape[3] // (3 * experts))
        me = lax.axis_index("expert").astype(jnp.int32).reshape(1)
        mod_weight = w_mod[0]
        lanes = -(-2 * experts // LANES) * LANES

        def payload(b):
            embed = level_embedding(levels[0, b], mod_weight.shape[0])
            modulation = jnp.dot(embed, mod_weight, preferred_element_type=jnp.float32)
            values = arrived[b].astype(jnp.float32)
            mean_square = jnp.mean(values * values, axis=1, keepdims=True)
            normed = (
                values * lax.rsqrt(mean_square + epsilon) * (1.0 + modulation[:, :features])
                + modulation[:, features:]
            ).astype(jnp.bfloat16)
            named = expert_ids[0, b][:, :, None] == jnp.arange(experts, dtype=jnp.int32)
            shares = jnp.sum(jnp.where(named, gate_values[0, b][:, :, None], 0.0), axis=1)
            high = lax.reduce_precision(shares, 8, 7)
            extra = jnp.concatenate([high, shares - high], axis=1).astype(jnp.bfloat16)
            extra = jnp.pad(extra, ((0, 0), (0, lanes - extra.shape[1])))
            return jnp.concatenate([normed, extra], axis=1)

        def added(a, b):
            return (a.astype(jnp.float32) + b.astype(jnp.float32)).astype(jnp.bfloat16)

        def tied(values):
            return lax.optimization_barrier(values)

        chains = [(b, step) for b in range(batches) for step in (1, -1)]
        first_half = (batches + 1) // 2
        top = {
            (b, step): far if not halved or (step == 1) == (b < first_half) else far - 1 for b, step in chains
        }
        part = tok_rows // 2 if halved else tok_rows
        kept = {1: slice(0, part), -1: slice(tok_rows - part, tok_rows)}
        own = [payload(b) for b in range(batches)]
        blocks = {(*chain, 0): own[chain[0]] for chain in chains}
        sums = {}

        def add_sums(keys):
            for key, value in zip(keys, group_sums(me, [blocks[key] for key in keys], weights, experts, room)):
                sums[key] = value

        waiting = []
        for k in range(1, far + 1):
            for b in range(batches):
                moving = [(b, step) for step in (1, -1) if top[b, step] >= k]
                sent = [blocks[(*chain, k - 1)] for chain in moving]
                if waiting and b == batches - 1:
                    sent, done = tied((sent, [sums[key] for key in waiting]))
                    sums.update(zip(waiting, done))
                    waiting = []
                blocks.update({(*chain, k): hop(value, chain[1]) for value, chain in zip(sent, moving)})
            if k == 1:
                first = [(*chain, 1) for chain in chains]
                got, weights = tied(([blocks[key] for key in first], in_vmem(weights)))
                blocks.update(zip(first, got))
            else:
                waiting = [(*c, k - 1) for c in chains if k < far or top[c] == far]
                waiting += [(b, 1, 0) for b in range(batches)] if k == 2 else []
                add_sums(waiting)

        add_sums([(*chain, top[chain]) for chain in chains])
        total = {}
        for chain in chains:
            step = chain[1]
            if not halved:
                value = sums[(*chain, far)]
            else:
                value = next(sums[chain[0], way, far] for way in (1, -1) if top[chain[0], way] == far)[kept[step]]
            for place in range(far - 1, -1, -1):
                value = hop(value, -step)
                near = sums[(*chain, place)] if place else None
                if place and halved and place == far - 1:
                    fresh = added(value, near[kept[step]])
                    value = jnp.concatenate(
                        [fresh, near[part:]] if step == 1 else [near[: tok_rows - part], fresh]
                    )
                elif place:
                    value = added(value, near)
            total[chain] = value
        results = []
        for b in range(batches):
            value = arrived[b].astype(jnp.float32) + sums[(b, 1, 0)].astype(jnp.float32)
            for step in (1, -1):
                value += total[b, step].astype(jnp.float32)
            results.append(value.astype(jnp.bfloat16))
        return jnp.stack(results)[None]

    return shards


def solution(mesh):
    placed = (
        P("section", None, "expert", None),
        P("section", None, "expert"),
        P("section", None, "expert", None),
        P("section", None, "expert", None),
        P("section", "expert", None, None),
        P("section", "expert", None, None),
        P("section", "expert", None, None),
        P("section", None, None),
    )
    return jax.shard_map(
        build(chip_cycle(mesh)),
        mesh=mesh,
        in_specs=placed,
        out_specs=P("section", None, "expert", None),
        check_vma=False,
    )
```

```python
import functools
import math

import jax
import jax.numpy as jnp
from jax import lax
from jax.experimental import pallas as pl
from jax.experimental.pallas import tpu as pltpu
from jax.sharding import PartitionSpec as P

epsilon = 1e-06
CORES = 2
LANES = 128
FF_CHUNK = 256
OUT_CHUNK = 512
CHUNK_BLOCKS = 4
VMEM_GRANT = 16 << 20


def level_embedding(levels, entries):
    half_width = entries // 2
    frequency = jnp.exp(-math.log(10000.0) * jnp.arange(half_width, dtype=jnp.float32) / half_width)
    angles = levels.astype(jnp.float32)[:, None] * frequency[None, :]
    return jnp.concatenate([jnp.cos(angles), jnp.sin(angles)], axis=1).astype(jnp.bfloat16)


def chip_cycle(mesh):
    line = list(mesh.devices.reshape(mesh.devices.shape[0], -1)[0])
    chips = len(line) // CORES
    places = [tuple(getattr(line[CORES * c], "coords", (0, 0, c))) for c in range(chips)]
    spans = [sorted({p[d] for p in places}) for d in range(3)]
    wide = [d for d in range(3) if len(spans[d]) > 1]
    if len(set(places)) != chips or len(wide) != 2 or math.prod(len(spans[d]) for d in wide) != chips:
        return list(range(chips))
    rows, cols = wide if len(spans[wide[0]]) % 2 == 0 else wide[::-1]
    if len(spans[rows]) % 2:
        return list(range(chips))
    if len(spans[rows]) > len(spans[cols]) and len(spans[cols]) % 2 == 0:
        rows, cols = cols, rows
    at = {(p[rows], p[cols]): c for c, p in enumerate(places)}
    order = []
    for i, r in enumerate(spans[rows]):
        along = spans[cols][1:]
        order += [(r, c) for c in (along if i % 2 == 0 else along[::-1])]
    order += [(r, spans[cols][0]) for r in reversed(spans[rows])]
    return [at[place] for place in order]


def chunk_of(extent, most):
    return next(c for c in range(min(extent, most), 0, -1) if extent % c == 0)


def dense_kernel(sizes, features, experts, ff, me_ref, *refs):
    count = len(sizes)
    blocks, weights = refs[:count], refs[count : count + 6]
    outs = refs[count + 6 : 2 * count + 6]
    rows, hidden = refs[2 * count + 6 :]
    ff_chunk, out_chunk = chunk_of(ff, FF_CHUNK), chunk_of(features, OUT_CHUNK)
    shares = [[], []]
    start = 0
    for block, size in zip(blocks, sizes):
        rows[start : start + size, :] = block[:, :features]
        extra = block[:, features:].astype(jnp.float32)
        lane = lax.broadcasted_iota(jnp.int32, extra.shape, 1)
        for i in range(CORES):
            expert = me_ref[0] ^ i
            named = (lane == expert) | (lane == expert + experts)
            shares[i].append(jnp.sum(jnp.where(named, extra, 0.0), axis=1, keepdims=True))
        start += size
    for i in range(CORES):
        share = jnp.concatenate(shares[i], axis=0)
        gate_weight, up_weight = weights[3 * i], weights[3 * i + 1]
        for c in range(0, ff, ff_chunk):
            part = slice(c, c + ff_chunk)
            gate = jnp.dot(rows[...], gate_weight[:, part], preferred_element_type=jnp.float32)
            up = jnp.dot(rows[...], up_weight[:, part], preferred_element_type=jnp.float32)
            value = gate / (1.0 + jnp.exp(-gate)) * up * share
            hidden[:, i * ff + c : i * ff + c + ff_chunk] = value.astype(jnp.bfloat16)
    for n in range(0, features, out_chunk):
        part = slice(n, n + out_chunk)
        total = jnp.dot(hidden[:, :ff], weights[2][:, part], preferred_element_type=jnp.float32)
        total += jnp.dot(hidden[:, ff:], weights[5][:, part], preferred_element_type=jnp.float32)
        total = total.astype(jnp.bfloat16)
        start = 0
        for out, size in zip(outs, sizes):
            out[:, part] = total[start : start + size]
            start += size


def picked_kernel(chunks, size, room, experts, me_ref, *refs):
    count = sum(chunks)
    blocks, weights = refs[:count], refs[count : count + 6]
    outs = refs[count + 6 : 2 * count + 6]
    picked, hidden, place = refs[2 * count + 6 :]
    features, ff = weights[0].shape
    ff_chunk, out_chunk = chunk_of(ff, FF_CHUNK), chunk_of(features, OUT_CHUNK)
    total = count * room
    shares = [[] for _ in range(CORES)]
    first = 0
    for chunk in chunks:
        tokens, slots = chunk * size, chunk * room
        values = jnp.concatenate([block[...] for block in blocks[first : first + chunk]], axis=0)
        extra = values[:, features:].astype(jnp.float32)
        lane = lax.broadcasted_iota(jnp.int32, extra.shape, 1)
        named = jnp.where(extra > 0.0, 1.0, 0.0)
        row = lax.broadcasted_iota(jnp.int32, (tokens, tokens), 0)
        column = lax.broadcasted_iota(jnp.int32, (tokens, tokens), 1)
        earlier = jnp.where((column < row) & (column // size == row // size), 1.0, 0.0)
        before = jnp.dot(
            earlier.astype(jnp.bfloat16), named.astype(jnp.bfloat16), preferred_element_type=jnp.float32
        )
        slot = lax.broadcasted_iota(jnp.int32, (tokens, slots), 1)
        start = lax.broadcasted_iota(jnp.int32, (tokens, slots), 0) // size * room
        for i in range(CORES):
            expert = me_ref[0] ^ i
            here = jnp.sum(jnp.where(lane == expert, before, 0.0), axis=1, keepdims=True)
            takes = jnp.sum(jnp.where(lane == expert, named, 0.0), axis=1, keepdims=True)
            match = (slot - start).astype(jnp.float32) == jnp.where(takes > 0.0, here, -1.0 * size * count)
            match = jnp.where(match, 1.0, 0.0).astype(jnp.bfloat16)
            place[first * size : first * size + tokens, i * slots : (i + 1) * slots] = match
            found = lax.dot_general(
                match, values, (((0,), (0,)), ((), ())), preferred_element_type=jnp.float32
            )
            at = i * total + first * room
            picked[at : at + slots, :] = found[:, :features].astype(jnp.bfloat16)
            both = lax.broadcasted_iota(jnp.int32, (slots, extra.shape[1]), 1)
            both = (both == expert) | (both == expert + experts)
            shares[i].append(jnp.sum(jnp.where(both, found[:, features:], 0.0), axis=1, keepdims=True))
        first += chunk
    for i in range(CORES):
        share = jnp.concatenate(shares[i], axis=0)
        gate_weight, up_weight = weights[3 * i], weights[3 * i + 1]
        rows = slice(i * total, (i + 1) * total)
        for c in range(0, ff, ff_chunk):
            part = slice(c, c + ff_chunk)
            gate = jnp.dot(picked[rows, :], gate_weight[:, part], preferred_element_type=jnp.float32)
            up = jnp.dot(picked[rows, :], up_weight[:, part], preferred_element_type=jnp.float32)
            value = gate / (1.0 + jnp.exp(-gate)) * up * share
            hidden[rows, part] = value.astype(jnp.bfloat16)
    for n in range(0, features, out_chunk):
        part = slice(n, n + out_chunk)
        made = [
            jnp.dot(
                hidden[i * total : (i + 1) * total, :],
                weights[3 * i + 2][:, part],
                preferred_element_type=jnp.float32,
            ).astype(jnp.bfloat16)
            for i in range(CORES)
        ]
        first = 0
        for chunk in chunks:
            tokens, slots = chunk * size, chunk * room
            mixed = jnp.concatenate([m[first * room : first * room + slots] for m in made], axis=0)
            spread = jnp.dot(
                place[first * size : first * size + tokens, : CORES * slots],
                mixed,
                preferred_element_type=jnp.float32,
            ).astype(jnp.bfloat16)
            for j in range(chunk):
                outs[first + j][:, part] = spread[j * size : (j + 1) * size]
            first += chunk


def load_kernel(*refs):
    count = len(refs) // 2
    sems = refs[2 * count]
    copies = [pltpu.make_async_copy(refs[i], refs[count + i], sems.at[i]) for i in range(count)]
    for copy in copies:
        copy.start()
    for copy in copies:
        copy.wait()


def in_vmem(values):
    return pl.pallas_call(
        load_kernel,
        out_shape=[pltpu.VMEM(value.shape, value.dtype) for value in values],
        in_specs=[pl.BlockSpec(memory_space=pltpu.HBM)] * len(values),
        out_specs=[pl.BlockSpec(memory_space=pltpu.VMEM)] * len(values),
        scratch_shapes=[pltpu.SemaphoreType.DMA((len(values),))],
        compiler_params=pltpu.CompilerParams(vmem_limit_bytes=1 << 20),
        cost_estimate=pl.CostEstimate(
            flops=0, bytes_accessed=0, transcendentals=0
        ),
    )(*[pltpu.with_memory_space_constraint(value, pltpu.HBM) for value in values])


def group_sums(me, blocks, weights, experts, room):
    count, size = len(blocks), blocks[0].shape[0]
    features, ff = weights[0].shape
    total = count * size
    if count >= CHUNK_BLOCKS:
        rows = count * room
        chunks = [min(CHUNK_BLOCKS, count - first) for first in range(0, count, CHUNK_BLOCKS)]
        kernel = functools.partial(picked_kernel, chunks, size, room, experts)
        scratch_shapes = [
            pltpu.VMEM((CORES * rows, features), jnp.bfloat16),
            pltpu.VMEM((CORES * rows, ff), jnp.bfloat16),
            pltpu.VMEM((total, CORES * CHUNK_BLOCKS * room), jnp.bfloat16),
        ]
    else:
        rows = total
        kernel = functools.partial(dense_kernel, [size] * count, features, experts, ff)
        scratch_shapes = [
            pltpu.VMEM((total, features), jnp.bfloat16),
            pltpu.VMEM((total, CORES * ff), jnp.bfloat16),
        ]
    near = pl.BlockSpec(memory_space=pltpu.VMEM)
    operands = [pltpu.with_memory_space_constraint(a, pltpu.VMEM) for a in (*blocks, *weights)]
    return pl.pallas_call(
        kernel,
        out_shape=[pltpu.VMEM((size, features), jnp.bfloat16)] * count,
        in_specs=[pl.BlockSpec(memory_space=pltpu.SMEM)] + [near] * len(operands),
        out_specs=[near] * count,
        scratch_shapes=scratch_shapes,
        compiler_params=pltpu.CompilerParams(vmem_limit_bytes=VMEM_GRANT),
        cost_estimate=pl.CostEstimate(
            flops=6 * CORES * rows * features * ff,
            bytes_accessed=4 * total * features,
            transcendentals=CORES * rows * ff,
        ),
    )(me, *operands)


def build(cycle):
    chips = len(cycle)
    experts = chips * CORES
    far = chips // 2
    halved = chips % 2 == 0

    def hop(value, step):
        pairs = [
            (cycle[i] * CORES + c, cycle[(i + step) % chips] * CORES + c)
            for i in range(chips)
            for c in range(CORES)
        ]
        return lax.ppermute(value, "expert", pairs)

    def swap(value):
        return lax.ppermute(value, "expert", [(i, i ^ 1) for i in range(experts)])

    def shards(emitted, levels, expert_ids, gate_values, w_gate, w_up, w_down, w_mod):
        sections = lax.axis_size("section")
        batches, tok_rows, features = emitted.shape[1:]
        half = tok_rows // 2
        around = [(s, (s + 1) % sections) for s in range(sections)]
        arrived = [lax.ppermute(emitted[0, b], "section", around) for b in range(batches)]
        mine = (w_gate[0, 0], w_up[0, 0], w_down[0, 0])
        gate_other, down_other = swap(mine[0]), swap(mine[2])
        up_mine, gate_other = lax.optimization_barrier((mine[1], gate_other))
        weights = (*mine, gate_other, swap(up_mine), down_other)
        room = min(tok_rows, 4 * tok_rows * expert_ids.shape[3] // (3 * experts))
        me = lax.axis_index("expert").astype(jnp.int32).reshape(1)
        mod_weight = w_mod[0]
        lanes = -(-2 * experts // LANES) * LANES

        def payload(b):
            embed = level_embedding(levels[0, b], mod_weight.shape[0])
            modulation = jnp.dot(embed, mod_weight, preferred_element_type=jnp.float32)
            values = arrived[b].astype(jnp.float32)
            mean_square = jnp.mean(values * values, axis=1, keepdims=True)
            normed = (
                values * lax.rsqrt(mean_square + epsilon) * (1.0 + modulation[:, :features])
                + modulation[:, features:]
            ).astype(jnp.bfloat16)
            named = expert_ids[0, b][:, :, None] == jnp.arange(experts, dtype=jnp.int32)
            shares = jnp.sum(jnp.where(named, gate_values[0, b][:, :, None], 0.0), axis=1)
            high = lax.reduce_precision(shares, 8, 7)
            extra = jnp.concatenate([high, shares - high], axis=1).astype(jnp.bfloat16)
            extra = jnp.pad(extra, ((0, 0), (0, lanes - extra.shape[1])))
            return jnp.concatenate([normed, extra], axis=1)

        def added(a, b):
            return (a.astype(jnp.float32) + b.astype(jnp.float32)).astype(jnp.bfloat16)

        def tied(values):
            return lax.optimization_barrier(values)

        chains = [(b, step) for b in range(batches) for step in (1, -1)]
        first_half = (batches + 1) // 2
        top = {
            (b, step): far if not halved or (step == 1) == (b < first_half) else far - 1 for b, step in chains
        }
        part = tok_rows // 2 if halved else tok_rows
        kept = {1: slice(0, part), -1: slice(tok_rows - part, tok_rows)}
        own = [payload(b) for b in range(batches)]
        blocks = {(*chain, 0): own[chain[0]] for chain in chains}
        sums = {}

        def add_sums(keys):
            for key, value in zip(keys, group_sums(me, [blocks[key] for key in keys], weights, experts, room)):
                sums[key] = value

        waiting = []
        for k in range(1, far + 1):
            for b in range(batches):
                moving = [(b, step) for step in (1, -1) if top[b, step] >= k]
                sent = [blocks[(*chain, k - 1)] for chain in moving]
                if waiting and b == batches - 1:
                    sent, done = tied((sent, [sums[key] for key in waiting]))
                    sums.update(zip(waiting, done))
                    waiting = []
                blocks.update({(*chain, k): hop(value, chain[1]) for value, chain in zip(sent, moving)})
            if k == 1:
                first = [(*chain, 1) for chain in chains]
                got, weights = tied(([blocks[key] for key in first], in_vmem(weights)))
                blocks.update(zip(first, got))
            else:
                waiting = [(*c, k - 1) for c in chains if k < far or top[c] == far]
                waiting += [(b, 1, 0) for b in range(batches)] if k == 2 else []
                add_sums(waiting)

        add_sums([(*chain, far) for chain in chains if top[chain] == far])
        if halved:
            add_sums([(*chain, far - 1) for chain in chains if top[chain] < far])
        total = {}
        for chain in chains:
            step = chain[1]
            if not halved:
                value = sums[(*chain, far)]
            else:
                value = next(sums[chain[0], way, far] for way in (1, -1) if top[chain[0], way] == far)[kept[step]]
            for place in range(far - 1, -1, -1):
                value = hop(value, -step)
                near = sums[(*chain, place)] if place else None
                if place and halved and place == far - 1:
                    fresh = added(value, near[kept[step]])
                    value = jnp.concatenate(
                        [fresh, near[part:]] if step == 1 else [near[: tok_rows - part], fresh]
                    )
                elif place:
                    value = added(value, near)
            total[chain] = value
        results = []
        for b in range(batches):
            value = arrived[b].astype(jnp.float32) + sums[(b, 1, 0)].astype(jnp.float32)
            for step in (1, -1):
                value += total[b, step].astype(jnp.float32)
            results.append(value.astype(jnp.bfloat16))
        return jnp.stack(results)[None]

    return shards


def solution(mesh):
    placed = (
        P("section", None, "expert", None),
        P("section", None, "expert"),
        P("section", None, "expert", None),
        P("section", None, "expert", None),
        P("section", "expert", None, None),
        P("section", "expert", None, None),
        P("section", "expert", None, None),
        P("section", None, None),
    )
    return jax.shard_map(
        build(chip_cycle(mesh)),
        mesh=mesh,
        in_specs=placed,
        out_specs=P("section", None, "expert", None),
        check_vma=False,
    )
```

```python
import functools
import math

import jax
import jax.numpy as jnp
from jax import lax
from jax.experimental import pallas as pl
from jax.experimental.pallas import tpu as pltpu
from jax.sharding import PartitionSpec as P

epsilon = 1e-06
CORES = 2
LANES = 128
FF_CHUNK = 256
OUT_CHUNK = 2048
CHUNK_BLOCKS = 4
VMEM_GRANT = 16 << 20


def level_embedding(levels, entries):
    half_width = entries // 2
    frequency = jnp.exp(-math.log(10000.0) * jnp.arange(half_width, dtype=jnp.float32) / half_width)
    angles = levels.astype(jnp.float32)[:, None] * frequency[None, :]
    return jnp.concatenate([jnp.cos(angles), jnp.sin(angles)], axis=1).astype(jnp.bfloat16)


def chip_cycle(mesh):
    line = list(mesh.devices.reshape(mesh.devices.shape[0], -1)[0])
    chips = len(line) // CORES
    places = [tuple(getattr(line[CORES * c], "coords", (0, 0, c))) for c in range(chips)]
    spans = [sorted({p[d] for p in places}) for d in range(3)]
    wide = [d for d in range(3) if len(spans[d]) > 1]
    if len(set(places)) != chips or len(wide) != 2 or math.prod(len(spans[d]) for d in wide) != chips:
        return list(range(chips))
    rows, cols = wide if len(spans[wide[0]]) % 2 == 0 else wide[::-1]
    if len(spans[rows]) % 2:
        return list(range(chips))
    if len(spans[rows]) > len(spans[cols]) and len(spans[cols]) % 2 == 0:
        rows, cols = cols, rows
    at = {(p[rows], p[cols]): c for c, p in enumerate(places)}
    order = []
    for i, r in enumerate(spans[rows]):
        along = spans[cols][1:]
        order += [(r, c) for c in (along if i % 2 == 0 else along[::-1])]
    order += [(r, spans[cols][0]) for r in reversed(spans[rows])]
    return [at[place] for place in order]


def chunk_of(extent, most):
    return next(c for c in range(min(extent, most), 0, -1) if extent % c == 0)


def dense_kernel(sizes, features, experts, ff, me_ref, *refs):
    count = len(sizes)
    blocks, weights = refs[:count], refs[count : count + 6]
    outs = refs[count + 6 : 2 * count + 6]
    rows, hidden = refs[2 * count + 6 :]
    ff_chunk, out_chunk = chunk_of(ff, FF_CHUNK), chunk_of(features, OUT_CHUNK)
    shares = [[], []]
    start = 0
    for block, size in zip(blocks, sizes):
        rows[start : start + size, :] = block[:, :features]
        extra = block[:, features:].astype(jnp.float32)
        lane = lax.broadcasted_iota(jnp.int32, extra.shape, 1)
        for i in range(CORES):
            expert = me_ref[0] ^ i
            named = (lane == expert) | (lane == expert + experts)
            shares[i].append(jnp.sum(jnp.where(named, extra, 0.0), axis=1, keepdims=True))
        start += size
    for i in range(CORES):
        share = jnp.concatenate(shares[i], axis=0)
        gate_weight, up_weight = weights[3 * i], weights[3 * i + 1]
        for c in range(0, ff, ff_chunk):
            part = slice(c, c + ff_chunk)
            gate = jnp.dot(rows[...], gate_weight[:, part], preferred_element_type=jnp.float32)
            up = jnp.dot(rows[...], up_weight[:, part], preferred_element_type=jnp.float32)
            value = gate / (1.0 + jnp.exp(-gate)) * up * share
            hidden[:, i * ff + c : i * ff + c + ff_chunk] = value.astype(jnp.bfloat16)
    for n in range(0, features, out_chunk):
        part = slice(n, n + out_chunk)
        total = jnp.dot(hidden[:, :ff], weights[2][:, part], preferred_element_type=jnp.float32)
        total += jnp.dot(hidden[:, ff:], weights[5][:, part], preferred_element_type=jnp.float32)
        total = total.astype(jnp.bfloat16)
        start = 0
        for out, size in zip(outs, sizes):
            out[:, part] = total[start : start + size]
            start += size


def picked_kernel(chunks, size, room, experts, me_ref, *refs):
    count = sum(chunks)
    blocks, weights = refs[:count], refs[count : count + 6]
    outs = refs[count + 6 : 2 * count + 6]
    picked, hidden, place = refs[2 * count + 6 :]
    features, ff = weights[0].shape
    ff_chunk, out_chunk = chunk_of(ff, FF_CHUNK), chunk_of(features, OUT_CHUNK)
    total = count * room
    shares = [[] for _ in range(CORES)]
    first = 0
    for chunk in chunks:
        tokens, slots = chunk * size, chunk * room
        values = jnp.concatenate([block[...] for block in blocks[first : first + chunk]], axis=0)
        extra = values[:, features:].astype(jnp.float32)
        lane = lax.broadcasted_iota(jnp.int32, extra.shape, 1)
        named = jnp.where(extra > 0.0, 1.0, 0.0)
        row = lax.broadcasted_iota(jnp.int32, (tokens, tokens), 0)
        column = lax.broadcasted_iota(jnp.int32, (tokens, tokens), 1)
        earlier = jnp.where((column < row) & (column // size == row // size), 1.0, 0.0)
        before = jnp.dot(
            earlier.astype(jnp.bfloat16), named.astype(jnp.bfloat16), preferred_element_type=jnp.float32
        )
        slot = lax.broadcasted_iota(jnp.int32, (tokens, slots), 1)
        start = lax.broadcasted_iota(jnp.int32, (tokens, slots), 0) // size * room
        for i in range(CORES):
            expert = me_ref[0] ^ i
            here = jnp.sum(jnp.where(lane == expert, before, 0.0), axis=1, keepdims=True)
            takes = jnp.sum(jnp.where(lane == expert, named, 0.0), axis=1, keepdims=True)
            match = (slot - start).astype(jnp.float32) == jnp.where(takes > 0.0, here, -1.0 * size * count)
            match = jnp.where(match, 1.0, 0.0).astype(jnp.bfloat16)
            place[first * size : first * size + tokens, i * slots : (i + 1) * slots] = match
            found = lax.dot_general(
                match, values, (((0,), (0,)), ((), ())), preferred_element_type=jnp.float32
            )
            at = i * total + first * room
            picked[at : at + slots, :] = found[:, :features].astype(jnp.bfloat16)
            both = lax.broadcasted_iota(jnp.int32, (slots, extra.shape[1]), 1)
            both = (both == expert) | (both == expert + experts)
            shares[i].append(jnp.sum(jnp.where(both, found[:, features:], 0.0), axis=1, keepdims=True))
        first += chunk
    for i in range(CORES):
        share = jnp.concatenate(shares[i], axis=0)
        gate_weight, up_weight = weights[3 * i], weights[3 * i + 1]
        rows = slice(i * total, (i + 1) * total)
        for c in range(0, ff, ff_chunk):
            part = slice(c, c + ff_chunk)
            gate = jnp.dot(picked[rows, :], gate_weight[:, part], preferred_element_type=jnp.float32)
            up = jnp.dot(picked[rows, :], up_weight[:, part], preferred_element_type=jnp.float32)
            value = gate / (1.0 + jnp.exp(-gate)) * up * share
            hidden[rows, part] = value.astype(jnp.bfloat16)
    for n in range(0, features, out_chunk):
        part = slice(n, n + out_chunk)
        made = [
            jnp.dot(
                hidden[i * total : (i + 1) * total, :],
                weights[3 * i + 2][:, part],
                preferred_element_type=jnp.float32,
            ).astype(jnp.bfloat16)
            for i in range(CORES)
        ]
        first = 0
        for chunk in chunks:
            tokens, slots = chunk * size, chunk * room
            mixed = jnp.concatenate([m[first * room : first * room + slots] for m in made], axis=0)
            spread = jnp.dot(
                place[first * size : first * size + tokens, : CORES * slots],
                mixed,
                preferred_element_type=jnp.float32,
            ).astype(jnp.bfloat16)
            for j in range(chunk):
                outs[first + j][:, part] = spread[j * size : (j + 1) * size]
            first += chunk


def load_kernel(*refs):
    count = len(refs) // 2
    sems = refs[2 * count]
    copies = [pltpu.make_async_copy(refs[i], refs[count + i], sems.at[i]) for i in range(count)]
    for copy in copies:
        copy.start()
    for copy in copies:
        copy.wait()


def in_vmem(values):
    return pl.pallas_call(
        load_kernel,
        out_shape=[pltpu.VMEM(value.shape, value.dtype) for value in values],
        in_specs=[pl.BlockSpec(memory_space=pltpu.HBM)] * len(values),
        out_specs=[pl.BlockSpec(memory_space=pltpu.VMEM)] * len(values),
        scratch_shapes=[pltpu.SemaphoreType.DMA((len(values),))],
        compiler_params=pltpu.CompilerParams(vmem_limit_bytes=1 << 20),
        cost_estimate=pl.CostEstimate(
            flops=0, bytes_accessed=0, transcendentals=0
        ),
    )(*[pltpu.with_memory_space_constraint(value, pltpu.HBM) for value in values])


def group_sums(me, blocks, weights, experts, room):
    count, size = len(blocks), blocks[0].shape[0]
    features, ff = weights[0].shape
    total = count * size
    if count >= CHUNK_BLOCKS:
        rows = count * room
        chunks = [min(CHUNK_BLOCKS, count - first) for first in range(0, count, CHUNK_BLOCKS)]
        kernel = functools.partial(picked_kernel, chunks, size, room, experts)
        scratch_shapes = [
            pltpu.VMEM((CORES * rows, features), jnp.bfloat16),
            pltpu.VMEM((CORES * rows, ff), jnp.bfloat16),
            pltpu.VMEM((total, CORES * CHUNK_BLOCKS * room), jnp.bfloat16),
        ]
    else:
        rows = total
        kernel = functools.partial(dense_kernel, [size] * count, features, experts, ff)
        scratch_shapes = [
            pltpu.VMEM((total, features), jnp.bfloat16),
            pltpu.VMEM((total, CORES * ff), jnp.bfloat16),
        ]
    near = pl.BlockSpec(memory_space=pltpu.VMEM)
    operands = [pltpu.with_memory_space_constraint(a, pltpu.VMEM) for a in (*blocks, *weights)]
    return pl.pallas_call(
        kernel,
        out_shape=[pltpu.VMEM((size, features), jnp.bfloat16)] * count,
        in_specs=[pl.BlockSpec(memory_space=pltpu.SMEM)] + [near] * len(operands),
        out_specs=[near] * count,
        scratch_shapes=scratch_shapes,
        compiler_params=pltpu.CompilerParams(vmem_limit_bytes=VMEM_GRANT),
        cost_estimate=pl.CostEstimate(
            flops=6 * CORES * rows * features * ff,
            bytes_accessed=4 * total * features,
            transcendentals=CORES * rows * ff,
        ),
    )(me, *operands)


def build(cycle):
    chips = len(cycle)
    experts = chips * CORES
    far = chips // 2
    halved = chips % 2 == 0

    def hop(value, step):
        pairs = [
            (cycle[i] * CORES + c, cycle[(i + step) % chips] * CORES + c)
            for i in range(chips)
            for c in range(CORES)
        ]
        return lax.ppermute(value, "expert", pairs)

    def swap(value):
        return lax.ppermute(value, "expert", [(i, i ^ 1) for i in range(experts)])

    def shards(emitted, levels, expert_ids, gate_values, w_gate, w_up, w_down, w_mod):
        sections = lax.axis_size("section")
        batches, tok_rows, features = emitted.shape[1:]
        half = tok_rows // 2
        around = [(s, (s + 1) % sections) for s in range(sections)]
        arrived = [lax.ppermute(emitted[0, b], "section", around) for b in range(batches)]
        mine = (w_gate[0, 0], w_up[0, 0], w_down[0, 0])
        gate_other, down_other = swap(mine[0]), swap(mine[2])
        up_mine, gate_other = lax.optimization_barrier((mine[1], gate_other))
        weights = (*mine, gate_other, swap(up_mine), down_other)
        room = min(tok_rows, 4 * tok_rows * expert_ids.shape[3] // (3 * experts))
        me = lax.axis_index("expert").astype(jnp.int32).reshape(1)
        mod_weight = w_mod[0]
        lanes = -(-2 * experts // LANES) * LANES

        def payload(b):
            embed = level_embedding(levels[0, b], mod_weight.shape[0])
            modulation = jnp.dot(embed, mod_weight, preferred_element_type=jnp.float32)
            values = arrived[b].astype(jnp.float32)
            mean_square = jnp.mean(values * values, axis=1, keepdims=True)
            normed = (
                values * lax.rsqrt(mean_square + epsilon) * (1.0 + modulation[:, :features])
                + modulation[:, features:]
            ).astype(jnp.bfloat16)
            named = expert_ids[0, b][:, :, None] == jnp.arange(experts, dtype=jnp.int32)
            shares = jnp.sum(jnp.where(named, gate_values[0, b][:, :, None], 0.0), axis=1)
            high = lax.reduce_precision(shares, 8, 7)
            extra = jnp.concatenate([high, shares - high], axis=1).astype(jnp.bfloat16)
            extra = jnp.pad(extra, ((0, 0), (0, lanes - extra.shape[1])))
            return jnp.concatenate([normed, extra], axis=1)

        def added(a, b):
            return (a.astype(jnp.float32) + b.astype(jnp.float32)).astype(jnp.bfloat16)

        def tied(values):
            return lax.optimization_barrier(values)

        chains = [(b, step) for b in range(batches) for step in (1, -1)]
        first_half = (batches + 1) // 2
        top = {
            (b, step): far if not halved or (step == 1) == (b < first_half) else far - 1 for b, step in chains
        }
        part = tok_rows // 2 if halved else tok_rows
        kept = {1: slice(0, part), -1: slice(tok_rows - part, tok_rows)}
        own = [payload(b) for b in range(batches)]
        blocks = {(*chain, 0): own[chain[0]] for chain in chains}
        sums = {}

        def add_sums(keys):
            for key, value in zip(keys, group_sums(me, [blocks[key] for key in keys], weights, experts, room)):
                sums[key] = value

        waiting = []
        for k in range(1, far + 1):
            for b in range(batches):
                moving = [(b, step) for step in (1, -1) if top[b, step] >= k]
                sent = [blocks[(*chain, k - 1)] for chain in moving]
                if waiting and b == batches - 1:
                    sent, done = tied((sent, [sums[key] for key in waiting]))
                    sums.update(zip(waiting, done))
                    waiting = []
                blocks.update({(*chain, k): hop(value, chain[1]) for value, chain in zip(sent, moving)})
            if k == 1:
                first = [(*chain, 1) for chain in chains]
                got, weights = tied(([blocks[key] for key in first], in_vmem(weights)))
                blocks.update(zip(first, got))
            else:
                waiting = [(*c, k - 1) for c in chains if k < far or top[c] == far]
                waiting += [(b, 1, 0) for b in range(batches)] if k == 2 else []
                add_sums(waiting)

        add_sums([(*chain, far) for chain in chains if top[chain] == far])
        if halved:
            add_sums([(*chain, far - 1) for chain in chains if top[chain] < far])
        total = {}
        for chain in chains:
            step = chain[1]
            if not halved:
                value = sums[(*chain, far)]
            else:
                value = next(sums[chain[0], way, far] for way in (1, -1) if top[chain[0], way] == far)[kept[step]]
            for place in range(far - 1, -1, -1):
                value = hop(value, -step)
                near = sums[(*chain, place)] if place else None
                if place and halved and place == far - 1:
                    fresh = added(value, near[kept[step]])
                    value = jnp.concatenate(
                        [fresh, near[part:]] if step == 1 else [near[: tok_rows - part], fresh]
                    )
                elif place:
                    value = added(value, near)
            total[chain] = value
        results = []
        for b in range(batches):
            value = arrived[b].astype(jnp.float32) + sums[(b, 1, 0)].astype(jnp.float32)
            for step in (1, -1):
                value += total[b, step].astype(jnp.float32)
            results.append(value.astype(jnp.bfloat16))
        return jnp.stack(results)[None]

    return shards


def solution(mesh):
    placed = (
        P("section", None, "expert", None),
        P("section", None, "expert"),
        P("section", None, "expert", None),
        P("section", None, "expert", None),
        P("section", "expert", None, None),
        P("section", "expert", None, None),
        P("section", "expert", None, None),
        P("section", None, None),
    )
    return jax.shard_map(
        build(chip_cycle(mesh)),
        mesh=mesh,
        in_specs=placed,
        out_specs=P("section", None, "expert", None),
        check_vma=False,
    )
```

```python
import functools
import math

import jax
import jax.numpy as jnp
from jax import lax
from jax.experimental import pallas as pl
from jax.experimental.pallas import tpu as pltpu
from jax.sharding import PartitionSpec as P

epsilon = 1e-06
CORES = 2
LANES = 128
FF_CHUNK = 256
OUT_CHUNK = 2048
CHUNK_BLOCKS = 4
VMEM_GRANT = 16 << 20


def level_embedding(levels, entries):
    half_width = entries // 2
    frequency = jnp.exp(-math.log(10000.0) * jnp.arange(half_width, dtype=jnp.float32) / half_width)
    angles = levels.astype(jnp.float32)[:, None] * frequency[None, :]
    return jnp.concatenate([jnp.cos(angles), jnp.sin(angles)], axis=1).astype(jnp.bfloat16)


def chip_cycle(mesh):
    line = list(mesh.devices.reshape(mesh.devices.shape[0], -1)[0])
    chips = len(line) // CORES
    places = [tuple(getattr(line[CORES * c], "coords", (0, 0, c))) for c in range(chips)]
    spans = [sorted({p[d] for p in places}) for d in range(3)]
    wide = [d for d in range(3) if len(spans[d]) > 1]
    if len(set(places)) != chips or len(wide) != 2 or math.prod(len(spans[d]) for d in wide) != chips:
        return list(range(chips))
    rows, cols = wide if len(spans[wide[0]]) % 2 == 0 else wide[::-1]
    if len(spans[rows]) % 2:
        return list(range(chips))
    if len(spans[rows]) > len(spans[cols]) and len(spans[cols]) % 2 == 0:
        rows, cols = cols, rows
    at = {(p[rows], p[cols]): c for c, p in enumerate(places)}
    order = []
    for i, r in enumerate(spans[rows]):
        along = spans[cols][1:]
        order += [(r, c) for c in (along if i % 2 == 0 else along[::-1])]
    order += [(r, spans[cols][0]) for r in reversed(spans[rows])]
    return [at[place] for place in order]


def chunk_of(extent, most):
    return next(c for c in range(min(extent, most), 0, -1) if extent % c == 0)


def dense_kernel(sizes, features, experts, ff, me_ref, *refs):
    count = len(sizes)
    blocks, weights = refs[:count], refs[count : count + 6]
    outs = refs[count + 6 : 2 * count + 6]
    rows, hidden = refs[2 * count + 6 :]
    ff_chunk, out_chunk = chunk_of(ff, FF_CHUNK), chunk_of(features, OUT_CHUNK)
    shares = [[], []]
    start = 0
    for block, size in zip(blocks, sizes):
        rows[start : start + size, :] = block[:, :features]
        extra = block[:, features:].astype(jnp.float32)
        lane = lax.broadcasted_iota(jnp.int32, extra.shape, 1)
        for i in range(CORES):
            expert = me_ref[0] ^ i
            named = (lane == expert) | (lane == expert + experts)
            shares[i].append(jnp.sum(jnp.where(named, extra, 0.0), axis=1, keepdims=True))
        start += size
    for i in range(CORES):
        share = jnp.concatenate(shares[i], axis=0)
        gate_weight, up_weight = weights[3 * i], weights[3 * i + 1]
        for c in range(0, ff, ff_chunk):
            part = slice(c, c + ff_chunk)
            gate = jnp.dot(rows[...], gate_weight[:, part], preferred_element_type=jnp.float32)
            up = jnp.dot(rows[...], up_weight[:, part], preferred_element_type=jnp.float32)
            value = gate / (1.0 + jnp.exp(-gate)) * up * share
            hidden[:, i * ff + c : i * ff + c + ff_chunk] = value.astype(jnp.bfloat16)
    for n in range(0, features, out_chunk):
        part = slice(n, n + out_chunk)
        total = jnp.dot(hidden[:, :ff], weights[2][:, part], preferred_element_type=jnp.float32)
        total += jnp.dot(hidden[:, ff:], weights[5][:, part], preferred_element_type=jnp.float32)
        total = total.astype(jnp.bfloat16)
        start = 0
        for out, size in zip(outs, sizes):
            out[:, part] = total[start : start + size]
            start += size


def picked_kernel(chunks, size, room, experts, me_ref, *refs):
    count = sum(chunks)
    blocks, weights = refs[:count], refs[count : count + 6]
    outs = refs[count + 6 : 2 * count + 6]
    picked, hidden, place = refs[2 * count + 6 :]
    features, ff = weights[0].shape
    ff_chunk, out_chunk = chunk_of(ff, FF_CHUNK), chunk_of(features, OUT_CHUNK)
    total = count * room
    shares = [[] for _ in range(CORES)]
    first = 0
    for chunk in chunks:
        tokens, slots = chunk * size, chunk * room
        values = jnp.concatenate([block[...] for block in blocks[first : first + chunk]], axis=0)
        extra = values[:, features:].astype(jnp.float32)
        lane = lax.broadcasted_iota(jnp.int32, extra.shape, 1)
        named = jnp.where(extra > 0.0, 1.0, 0.0)
        row = lax.broadcasted_iota(jnp.int32, (tokens, tokens), 0)
        column = lax.broadcasted_iota(jnp.int32, (tokens, tokens), 1)
        earlier = jnp.where((column < row) & (column // size == row // size), 1.0, 0.0)
        before = jnp.dot(
            earlier.astype(jnp.bfloat16), named.astype(jnp.bfloat16), preferred_element_type=jnp.float32
        )
        slot = lax.broadcasted_iota(jnp.int32, (tokens, slots), 1)
        start = lax.broadcasted_iota(jnp.int32, (tokens, slots), 0) // size * room
        for i in range(CORES):
            expert = me_ref[0] ^ i
            here = jnp.sum(jnp.where(lane == expert, before, 0.0), axis=1, keepdims=True)
            takes = jnp.sum(jnp.where(lane == expert, named, 0.0), axis=1, keepdims=True)
            match = (slot - start).astype(jnp.float32) == jnp.where(takes > 0.0, here, -1.0 * size * count)
            match = jnp.where(match, 1.0, 0.0).astype(jnp.bfloat16)
            place[first * size : first * size + tokens, i * slots : (i + 1) * slots] = match
            found = lax.dot_general(
                match, values, (((0,), (0,)), ((), ())), preferred_element_type=jnp.float32
            )
            at = i * total + first * room
            picked[at : at + slots, :] = found[:, :features].astype(jnp.bfloat16)
            both = lax.broadcasted_iota(jnp.int32, (slots, extra.shape[1]), 1)
            both = (both == expert) | (both == expert + experts)
            shares[i].append(jnp.sum(jnp.where(both, found[:, features:], 0.0), axis=1, keepdims=True))
        first += chunk
    for i in range(CORES):
        share = jnp.concatenate(shares[i], axis=0)
        gate_weight, up_weight = weights[3 * i], weights[3 * i + 1]
        rows = slice(i * total, (i + 1) * total)
        for c in range(0, ff, ff_chunk):
            part = slice(c, c + ff_chunk)
            gate = jnp.dot(picked[rows, :], gate_weight[:, part], preferred_element_type=jnp.float32)
            up = jnp.dot(picked[rows, :], up_weight[:, part], preferred_element_type=jnp.float32)
            value = gate / (1.0 + jnp.exp(-gate)) * up * share
            hidden[rows, part] = value.astype(jnp.bfloat16)
    for n in range(0, features, out_chunk):
        part = slice(n, n + out_chunk)
        made = [
            jnp.dot(
                hidden[i * total : (i + 1) * total, :],
                weights[3 * i + 2][:, part],
                preferred_element_type=jnp.float32,
            ).astype(jnp.bfloat16)
            for i in range(CORES)
        ]
        first = 0
        for chunk in chunks:
            tokens, slots = chunk * size, chunk * room
            mixed = jnp.concatenate([m[first * room : first * room + slots] for m in made], axis=0)
            spread = jnp.dot(
                place[first * size : first * size + tokens, : CORES * slots],
                mixed,
                preferred_element_type=jnp.float32,
            ).astype(jnp.bfloat16)
            for j in range(chunk):
                outs[first + j][:, part] = spread[j * size : (j + 1) * size]
            first += chunk


def load_kernel(*refs):
    count = len(refs) // 2
    sems = refs[2 * count]
    copies = [pltpu.make_async_copy(refs[i], refs[count + i], sems.at[i]) for i in range(count)]
    for copy in copies:
        copy.start()
    for copy in copies:
        copy.wait()


def in_vmem(values):
    return pl.pallas_call(
        load_kernel,
        out_shape=[pltpu.VMEM(value.shape, value.dtype) for value in values],
        in_specs=[pl.BlockSpec(memory_space=pltpu.HBM)] * len(values),
        out_specs=[pl.BlockSpec(memory_space=pltpu.VMEM)] * len(values),
        scratch_shapes=[pltpu.SemaphoreType.DMA((len(values),))],
        compiler_params=pltpu.CompilerParams(vmem_limit_bytes=1 << 20),
        cost_estimate=pl.CostEstimate(
            flops=0, bytes_accessed=0, transcendentals=0
        ),
    )(*[pltpu.with_memory_space_constraint(value, pltpu.HBM) for value in values])


def group_sums(me, blocks, weights, experts, room):
    count, size = len(blocks), blocks[0].shape[0]
    features, ff = weights[0].shape
    total = count * size
    if count >= CHUNK_BLOCKS:
        rows = count * room
        chunks = [min(CHUNK_BLOCKS, count - first) for first in range(0, count, CHUNK_BLOCKS)]
        kernel = functools.partial(picked_kernel, chunks, size, room, experts)
        scratch_shapes = [
            pltpu.VMEM((CORES * rows, features), jnp.bfloat16),
            pltpu.VMEM((CORES * rows, ff), jnp.bfloat16),
            pltpu.VMEM((total, CORES * CHUNK_BLOCKS * room), jnp.bfloat16),
        ]
    else:
        rows = total
        kernel = functools.partial(dense_kernel, [size] * count, features, experts, ff)
        scratch_shapes = [
            pltpu.VMEM((total, features), jnp.bfloat16),
            pltpu.VMEM((total, CORES * ff), jnp.bfloat16),
        ]
    near = pl.BlockSpec(memory_space=pltpu.VMEM)
    operands = [pltpu.with_memory_space_constraint(a, pltpu.VMEM) for a in (*blocks, *weights)]
    return pl.pallas_call(
        kernel,
        out_shape=[pltpu.VMEM((size, features), jnp.bfloat16)] * count,
        in_specs=[pl.BlockSpec(memory_space=pltpu.SMEM)] + [near] * len(operands),
        out_specs=[near] * count,
        scratch_shapes=scratch_shapes,
        compiler_params=pltpu.CompilerParams(vmem_limit_bytes=VMEM_GRANT),
        cost_estimate=pl.CostEstimate(
            flops=6 * CORES * rows * features * ff,
            bytes_accessed=4 * total * features,
            transcendentals=CORES * rows * ff,
        ),
    )(me, *operands)


def final_kernel(count, *refs):
    out, made, sems = refs[-3:]
    copies = []
    rows = made.shape[1]
    size = rows // 2 if rows % 32 == 0 else rows
    for b in range(count):
        for first in range(0, rows, size):
            part = slice(first, first + size)
            total = sum(ref[part, :].astype(jnp.float32) for ref in refs[b * 4 : b * 4 + 4])
            made[b, part, :] = total.astype(jnp.bfloat16)
            copies.append(
                pltpu.make_async_copy(made.at[b, part, :], out.at[b, part, :], sems.at[len(copies)])
            )
            copies[-1].start()
    for copy in copies:
        copy.wait()


def final_sums(parts):
    count, (rows, features) = len(parts), parts[0][0].shape
    near = pl.BlockSpec(memory_space=pltpu.VMEM)
    return pl.pallas_call(
        functools.partial(final_kernel, count),
        out_shape=jax.ShapeDtypeStruct((count, rows, features), jnp.bfloat16),
        in_specs=[near] * (4 * count),
        out_specs=pl.BlockSpec(memory_space=pl.ANY),
        scratch_shapes=[
            pltpu.VMEM((count, rows, features), jnp.bfloat16),
            pltpu.SemaphoreType.DMA((2 * count,)),
        ],
        compiler_params=pltpu.CompilerParams(vmem_limit_bytes=VMEM_GRANT),
    )(*[value for part in parts for value in part])


def build(cycle):
    chips = len(cycle)
    experts = chips * CORES
    far = chips // 2
    halved = chips % 2 == 0

    def hop(value, step):
        pairs = [
            (cycle[i] * CORES + c, cycle[(i + step) % chips] * CORES + c)
            for i in range(chips)
            for c in range(CORES)
        ]
        return lax.ppermute(value, "expert", pairs)

    def swap(value):
        return lax.ppermute(value, "expert", [(i, i ^ 1) for i in range(experts)])

    def shards(emitted, levels, expert_ids, gate_values, w_gate, w_up, w_down, w_mod):
        sections = lax.axis_size("section")
        batches, tok_rows, features = emitted.shape[1:]
        half = tok_rows // 2
        around = [(s, (s + 1) % sections) for s in range(sections)]
        arrived = [lax.ppermute(emitted[0, b], "section", around) for b in range(batches)]
        mine = (w_gate[0, 0], w_up[0, 0], w_down[0, 0])
        gate_other, down_other = swap(mine[0]), swap(mine[2])
        up_mine, gate_other = lax.optimization_barrier((mine[1], gate_other))
        weights = (*mine, gate_other, swap(up_mine), down_other)
        room = min(tok_rows, 4 * tok_rows * expert_ids.shape[3] // (3 * experts))
        me = lax.axis_index("expert").astype(jnp.int32).reshape(1)
        mod_weight = w_mod[0]
        lanes = -(-2 * experts // LANES) * LANES

        def payload(b):
            embed = level_embedding(levels[0, b], mod_weight.shape[0])
            modulation = jnp.dot(embed, mod_weight, preferred_element_type=jnp.float32)
            values = arrived[b].astype(jnp.float32)
            mean_square = jnp.mean(values * values, axis=1, keepdims=True)
            normed = (
                values * lax.rsqrt(mean_square + epsilon) * (1.0 + modulation[:, :features])
                + modulation[:, features:]
            ).astype(jnp.bfloat16)
            named = expert_ids[0, b][:, :, None] == jnp.arange(experts, dtype=jnp.int32)
            shares = jnp.sum(jnp.where(named, gate_values[0, b][:, :, None], 0.0), axis=1)
            high = lax.reduce_precision(shares, 8, 7)
            extra = jnp.concatenate([high, shares - high], axis=1).astype(jnp.bfloat16)
            extra = jnp.pad(extra, ((0, 0), (0, lanes - extra.shape[1])))
            return jnp.concatenate([normed, extra], axis=1)

        def added(a, b):
            return (a.astype(jnp.float32) + b.astype(jnp.float32)).astype(jnp.bfloat16)

        def tied(values):
            return lax.optimization_barrier(values)

        chains = [(b, step) for b in range(batches) for step in (1, -1)]
        first_half = (batches + 1) // 2
        top = {
            (b, step): far if not halved or (step == 1) == (b < first_half) else far - 1 for b, step in chains
        }
        part = tok_rows // 2 if halved else tok_rows
        kept = {1: slice(0, part), -1: slice(tok_rows - part, tok_rows)}
        own = [payload(b) for b in range(batches)]
        blocks = {(*chain, 0): own[chain[0]] for chain in chains}
        sums = {}

        def add_sums(keys):
            for key, value in zip(keys, group_sums(me, [blocks[key] for key in keys], weights, experts, room)):
                sums[key] = value

        waiting = []
        for k in range(1, far + 1):
            for b in range(batches):
                moving = [(b, step) for step in (1, -1) if top[b, step] >= k]
                sent = [blocks[(*chain, k - 1)] for chain in moving]
                if waiting and b == batches - 1:
                    sent, done = tied((sent, [sums[key] for key in waiting]))
                    sums.update(zip(waiting, done))
                    waiting = []
                blocks.update({(*chain, k): hop(value, chain[1]) for value, chain in zip(sent, moving)})
            if k == 1:
                first = [(*chain, 1) for chain in chains]
                got, weights = tied(([blocks[key] for key in first], in_vmem(weights)))
                blocks.update(zip(first, got))
            else:
                waiting = [(*c, k - 1) for c in chains if k < far or top[c] == far]
                waiting += [(b, 1, 0) for b in range(batches)] if k == 2 else []
                add_sums(waiting)

        add_sums([(*chain, far) for chain in chains if top[chain] == far])
        if halved:
            add_sums([(*chain, far - 1) for chain in chains if top[chain] < far])
        total = {}
        for chain in chains:
            step = chain[1]
            if not halved:
                value = sums[(*chain, far)]
            else:
                value = next(sums[chain[0], way, far] for way in (1, -1) if top[chain[0], way] == far)[kept[step]]
            for place in range(far - 1, -1, -1):
                value = hop(value, -step)
                near = sums[(*chain, place)] if place else None
                if place and halved and place == far - 1:
                    fresh = added(value, near[kept[step]])
                    value = jnp.concatenate(
                        [fresh, near[part:]] if step == 1 else [near[: tok_rows - part], fresh]
                    )
                elif place:
                    value = added(value, near)
            total[chain] = value
        parts = [
            (arrived[b], sums[b, 1, 0], total[b, 1], total[b, -1]) for b in range(batches)
        ]
        return final_sums(parts)[None]

    return shards


def solution(mesh):
    placed = (
        P("section", None, "expert", None),
        P("section", None, "expert"),
        P("section", None, "expert", None),
        P("section", None, "expert", None),
        P("section", "expert", None, None),
        P("section", "expert", None, None),
        P("section", "expert", None, None),
        P("section", None, None),
    )
    return jax.shard_map(
        build(chip_cycle(mesh)),
        mesh=mesh,
        in_specs=placed,
        out_specs=P("section", None, "expert", None),
        check_vma=False,
    )
```

```python
import functools
import math

import jax
import jax.numpy as jnp
from jax import lax
from jax.experimental import pallas as pl
from jax.experimental.pallas import tpu as pltpu
from jax.sharding import PartitionSpec as P

epsilon = 1e-06
CORES = 2
LANES = 128
FF_CHUNK = 256
OUT_CHUNK = 2048
CHUNK_BLOCKS = 4
VMEM_GRANT = 16 << 20


def level_embedding(levels, entries):
    half_width = entries // 2
    frequency = jnp.exp(-math.log(10000.0) * jnp.arange(half_width, dtype=jnp.float32) / half_width)
    angles = levels.astype(jnp.float32)[:, None] * frequency[None, :]
    return jnp.concatenate([jnp.cos(angles), jnp.sin(angles)], axis=1).astype(jnp.bfloat16)


def chip_cycle(mesh):
    line = list(mesh.devices.reshape(mesh.devices.shape[0], -1)[0])
    chips = len(line) // CORES
    places = [tuple(getattr(line[CORES * c], "coords", (0, 0, c))) for c in range(chips)]
    spans = [sorted({p[d] for p in places}) for d in range(3)]
    wide = [d for d in range(3) if len(spans[d]) > 1]
    if len(set(places)) != chips or len(wide) != 2 or math.prod(len(spans[d]) for d in wide) != chips:
        return list(range(chips))
    rows, cols = wide if len(spans[wide[0]]) % 2 == 0 else wide[::-1]
    if len(spans[rows]) % 2:
        return list(range(chips))
    if len(spans[rows]) > len(spans[cols]) and len(spans[cols]) % 2 == 0:
        rows, cols = cols, rows
    at = {(p[rows], p[cols]): c for c, p in enumerate(places)}
    order = []
    for i, r in enumerate(spans[rows]):
        along = spans[cols][1:]
        order += [(r, c) for c in (along if i % 2 == 0 else along[::-1])]
    order += [(r, spans[cols][0]) for r in reversed(spans[rows])]
    return [at[place] for place in order]


def chunk_of(extent, most):
    return next(c for c in range(min(extent, most), 0, -1) if extent % c == 0)


def dense_kernel(sizes, features, experts, ff, me_ref, *refs):
    count = len(sizes)
    blocks, weights = refs[:count], refs[count : count + 6]
    outs = refs[count + 6 : 2 * count + 6]
    rows, hidden = refs[2 * count + 6 :]
    ff_chunk, out_chunk = chunk_of(ff, FF_CHUNK), chunk_of(features, OUT_CHUNK)
    shares = [[], []]
    start = 0
    for block, size in zip(blocks, sizes):
        rows[start : start + size, :] = block[:, :features]
        extra = block[:, features:].astype(jnp.float32)
        lane = lax.broadcasted_iota(jnp.int32, extra.shape, 1)
        for i in range(CORES):
            expert = me_ref[0] ^ i
            named = (lane == expert) | (lane == expert + experts)
            shares[i].append(jnp.sum(jnp.where(named, extra, 0.0), axis=1, keepdims=True))
        start += size
    for i in range(CORES):
        share = jnp.concatenate(shares[i], axis=0)
        gate_weight, up_weight = weights[3 * i], weights[3 * i + 1]
        for c in range(0, ff, ff_chunk):
            part = slice(c, c + ff_chunk)
            gate = jnp.dot(rows[...], gate_weight[:, part], preferred_element_type=jnp.float32)
            up = jnp.dot(rows[...], up_weight[:, part], preferred_element_type=jnp.float32)
            value = gate / (1.0 + jnp.exp(-gate)) * up * share
            hidden[:, i * ff + c : i * ff + c + ff_chunk] = value.astype(jnp.bfloat16)
    for n in range(0, features, out_chunk):
        part = slice(n, n + out_chunk)
        total = jnp.dot(hidden[:, :ff], weights[2][:, part], preferred_element_type=jnp.float32)
        total += jnp.dot(hidden[:, ff:], weights[5][:, part], preferred_element_type=jnp.float32)
        total = total.astype(jnp.bfloat16)
        start = 0
        for out, size in zip(outs, sizes):
            out[:, part] = total[start : start + size]
            start += size


def picked_kernel(chunks, size, room, experts, me_ref, *refs):
    count = sum(chunks)
    blocks, weights = refs[:count], refs[count : count + 6]
    outs = refs[count + 6 : 2 * count + 6]
    picked, hidden, place = refs[2 * count + 6 :]
    features, ff = weights[0].shape
    ff_chunk, out_chunk = chunk_of(ff, FF_CHUNK), chunk_of(features, OUT_CHUNK)
    total = count * room
    shares = [[] for _ in range(CORES)]
    first = 0
    for chunk in chunks:
        tokens, slots = chunk * size, chunk * room
        values = jnp.concatenate([block[...] for block in blocks[first : first + chunk]], axis=0)
        extra = values[:, features:].astype(jnp.float32)
        lane = lax.broadcasted_iota(jnp.int32, extra.shape, 1)
        named = jnp.where(extra > 0.0, 1.0, 0.0)
        row = lax.broadcasted_iota(jnp.int32, (tokens, tokens), 0)
        column = lax.broadcasted_iota(jnp.int32, (tokens, tokens), 1)
        earlier = jnp.where((column < row) & (column // size == row // size), 1.0, 0.0)
        before = jnp.dot(
            earlier.astype(jnp.bfloat16), named.astype(jnp.bfloat16), preferred_element_type=jnp.float32
        )
        slot = lax.broadcasted_iota(jnp.int32, (tokens, slots), 1)
        start = lax.broadcasted_iota(jnp.int32, (tokens, slots), 0) // size * room
        for i in range(CORES):
            expert = me_ref[0] ^ i
            here = jnp.sum(jnp.where(lane == expert, before, 0.0), axis=1, keepdims=True)
            takes = jnp.sum(jnp.where(lane == expert, named, 0.0), axis=1, keepdims=True)
            match = (slot - start).astype(jnp.float32) == jnp.where(takes > 0.0, here, -1.0 * size * count)
            match = jnp.where(match, 1.0, 0.0).astype(jnp.bfloat16)
            place[first * size : first * size + tokens, i * slots : (i + 1) * slots] = match
            found = lax.dot_general(
                match, values, (((0,), (0,)), ((), ())), preferred_element_type=jnp.float32
            )
            at = i * total + first * room
            picked[at : at + slots, :] = found[:, :features].astype(jnp.bfloat16)
            both = lax.broadcasted_iota(jnp.int32, (slots, extra.shape[1]), 1)
            both = (both == expert) | (both == expert + experts)
            shares[i].append(jnp.sum(jnp.where(both, found[:, features:], 0.0), axis=1, keepdims=True))
        first += chunk
    for i in range(CORES):
        share = jnp.concatenate(shares[i], axis=0)
        gate_weight, up_weight = weights[3 * i], weights[3 * i + 1]
        rows = slice(i * total, (i + 1) * total)
        for c in range(0, ff, ff_chunk):
            part = slice(c, c + ff_chunk)
            gate = jnp.dot(picked[rows, :], gate_weight[:, part], preferred_element_type=jnp.float32)
            up = jnp.dot(picked[rows, :], up_weight[:, part], preferred_element_type=jnp.float32)
            value = gate / (1.0 + jnp.exp(-gate)) * up * share
            hidden[rows, part] = value.astype(jnp.bfloat16)
    for n in range(0, features, out_chunk):
        part = slice(n, n + out_chunk)
        made = [
            jnp.dot(
                hidden[i * total : (i + 1) * total, :],
                weights[3 * i + 2][:, part],
                preferred_element_type=jnp.float32,
            ).astype(jnp.bfloat16)
            for i in range(CORES)
        ]
        first = 0
        for chunk in chunks:
            tokens, slots = chunk * size, chunk * room
            mixed = jnp.concatenate([m[first * room : first * room + slots] for m in made], axis=0)
            spread = jnp.dot(
                place[first * size : first * size + tokens, : CORES * slots],
                mixed,
                preferred_element_type=jnp.float32,
            ).astype(jnp.bfloat16)
            for j in range(chunk):
                outs[first + j][:, part] = spread[j * size : (j + 1) * size]
            first += chunk


def load_kernel(*refs):
    count = len(refs) // 2
    sems = refs[2 * count]
    copies = [pltpu.make_async_copy(refs[i], refs[count + i], sems.at[i]) for i in range(count)]
    for copy in copies:
        copy.start()
    for copy in copies:
        copy.wait()


def in_vmem(values):
    return pl.pallas_call(
        load_kernel,
        out_shape=[pltpu.VMEM(value.shape, value.dtype) for value in values],
        in_specs=[pl.BlockSpec(memory_space=pltpu.HBM)] * len(values),
        out_specs=[pl.BlockSpec(memory_space=pltpu.VMEM)] * len(values),
        scratch_shapes=[pltpu.SemaphoreType.DMA((len(values),))],
        compiler_params=pltpu.CompilerParams(vmem_limit_bytes=1 << 20),
        cost_estimate=pl.CostEstimate(
            flops=0, bytes_accessed=0, transcendentals=0
        ),
    )(*[pltpu.with_memory_space_constraint(value, pltpu.HBM) for value in values])


def group_sums(me, blocks, weights, experts, room):
    count, size = len(blocks), blocks[0].shape[0]
    features, ff = weights[0].shape
    total = count * size
    if count >= CHUNK_BLOCKS:
        rows = count * room
        chunks = [min(CHUNK_BLOCKS, count - first) for first in range(0, count, CHUNK_BLOCKS)]
        kernel = functools.partial(picked_kernel, chunks, size, room, experts)
        scratch_shapes = [
            pltpu.VMEM((CORES * rows, features), jnp.bfloat16),
            pltpu.VMEM((CORES * rows, ff), jnp.bfloat16),
            pltpu.VMEM((total, CORES * CHUNK_BLOCKS * room), jnp.bfloat16),
        ]
    else:
        rows = total
        kernel = functools.partial(dense_kernel, [size] * count, features, experts, ff)
        scratch_shapes = [
            pltpu.VMEM((total, features), jnp.bfloat16),
            pltpu.VMEM((total, CORES * ff), jnp.bfloat16),
        ]
    near = pl.BlockSpec(memory_space=pltpu.VMEM)
    operands = [pltpu.with_memory_space_constraint(a, pltpu.VMEM) for a in (*blocks, *weights)]
    return pl.pallas_call(
        kernel,
        out_shape=[pltpu.VMEM((size, features), jnp.bfloat16)] * count,
        in_specs=[pl.BlockSpec(memory_space=pltpu.SMEM)] + [near] * len(operands),
        out_specs=[near] * count,
        scratch_shapes=scratch_shapes,
        compiler_params=pltpu.CompilerParams(vmem_limit_bytes=VMEM_GRANT),
        cost_estimate=pl.CostEstimate(
            flops=6 * CORES * rows * features * ff,
            bytes_accessed=4 * total * features,
            transcendentals=CORES * rows * ff,
        ),
    )(me, *operands)


def final_kernel(count, *refs):
    out, made, sems = refs[-3:]
    copies = []
    rows = made.shape[1]
    size = rows // 2 if rows % 32 == 0 else rows
    for b in range(count):
        for first in range(0, rows, size):
            part = slice(first, first + size)
            total = sum(ref[part, :].astype(jnp.float32) for ref in refs[b * 4 : b * 4 + 4])
            made[b, part, :] = total.astype(jnp.bfloat16)
            copies.append(
                pltpu.make_async_copy(made.at[b, part, :], out.at[b, part, :], sems.at[len(copies)])
            )
            copies[-1].start()
    for copy in copies:
        copy.wait()


def final_sums(parts):
    count, (rows, features) = len(parts), parts[0][0].shape
    near = pl.BlockSpec(memory_space=pltpu.VMEM)
    return pl.pallas_call(
        functools.partial(final_kernel, count),
        out_shape=jax.ShapeDtypeStruct((count, rows, features), jnp.bfloat16),
        in_specs=[near] * (4 * count),
        out_specs=pl.BlockSpec(memory_space=pl.ANY),
        scratch_shapes=[
            pltpu.VMEM((count, rows, features), jnp.bfloat16),
            pltpu.SemaphoreType.DMA((2 * count,)),
        ],
        compiler_params=pltpu.CompilerParams(vmem_limit_bytes=VMEM_GRANT),
    )(*[value for part in parts for value in part])


def build(cycle):
    chips = len(cycle)
    experts = chips * CORES
    far = chips // 2
    halved = chips % 2 == 0

    def hop(value, step):
        pairs = [
            (cycle[i] * CORES + c, cycle[(i + step) % chips] * CORES + c)
            for i in range(chips)
            for c in range(CORES)
        ]
        return lax.ppermute(value, "expert", pairs)

    def swap(value):
        return lax.ppermute(value, "expert", [(i, i ^ 1) for i in range(experts)])

    def shards(emitted, levels, expert_ids, gate_values, w_gate, w_up, w_down, w_mod):
        sections = lax.axis_size("section")
        batches, tok_rows, features = emitted.shape[1:]
        half = tok_rows // 2
        around = [(s, (s + 1) % sections) for s in range(sections)]
        arrived = [lax.ppermute(emitted[0, b], "section", around) for b in range(batches)]
        mine = (w_gate[0, 0], w_up[0, 0], w_down[0, 0])
        gate_other, up_other = swap(mine[0]), swap(mine[1])
        down_mine, gate_other = lax.optimization_barrier((mine[2], gate_other))
        weights = (*mine, gate_other, up_other, swap(down_mine))
        room = min(tok_rows, 4 * tok_rows * expert_ids.shape[3] // (3 * experts))
        me = lax.axis_index("expert").astype(jnp.int32).reshape(1)
        mod_weight = w_mod[0]
        lanes = -(-2 * experts // LANES) * LANES

        def payload(b):
            embed = level_embedding(levels[0, b], mod_weight.shape[0])
            modulation = jnp.dot(embed, mod_weight, preferred_element_type=jnp.float32)
            values = arrived[b].astype(jnp.float32)
            mean_square = jnp.mean(values * values, axis=1, keepdims=True)
            normed = (
                values * lax.rsqrt(mean_square + epsilon) * (1.0 + modulation[:, :features])
                + modulation[:, features:]
            ).astype(jnp.bfloat16)
            named = expert_ids[0, b][:, :, None] == jnp.arange(experts, dtype=jnp.int32)
            shares = jnp.sum(jnp.where(named, gate_values[0, b][:, :, None], 0.0), axis=1)
            high = lax.reduce_precision(shares, 8, 7)
            extra = jnp.concatenate([high, shares - high], axis=1).astype(jnp.bfloat16)
            extra = jnp.pad(extra, ((0, 0), (0, lanes - extra.shape[1])))
            return jnp.concatenate([normed, extra], axis=1)

        def added(a, b):
            return (a.astype(jnp.float32) + b.astype(jnp.float32)).astype(jnp.bfloat16)

        def tied(values):
            return lax.optimization_barrier(values)

        chains = [(b, step) for b in range(batches) for step in (1, -1)]
        first_half = (batches + 1) // 2
        top = {
            (b, step): far if not halved or (step == 1) == (b < first_half) else far - 1 for b, step in chains
        }
        part = tok_rows // 2 if halved else tok_rows
        kept = {1: slice(0, part), -1: slice(tok_rows - part, tok_rows)}
        own = [payload(b) for b in range(batches)]
        blocks = {(*chain, 0): own[chain[0]] for chain in chains}
        sums = {}

        def add_sums(keys):
            for key, value in zip(keys, group_sums(me, [blocks[key] for key in keys], weights, experts, room)):
                sums[key] = value

        waiting = []
        for k in range(1, far + 1):
            for b in range(batches):
                moving = [(b, step) for step in (1, -1) if top[b, step] >= k]
                sent = [blocks[(*chain, k - 1)] for chain in moving]
                if waiting and b == batches - 1:
                    sent, done = tied((sent, [sums[key] for key in waiting]))
                    sums.update(zip(waiting, done))
                    waiting = []
                blocks.update({(*chain, k): hop(value, chain[1]) for value, chain in zip(sent, moving)})
            if k == 1:
                first = [(*chain, 1) for chain in chains]
                got, weights = tied(([blocks[key] for key in first], in_vmem(weights)))
                blocks.update(zip(first, got))
            else:
                waiting = [(*c, k - 1) for c in chains if k < far or top[c] == far]
                waiting += [(b, 1, 0) for b in range(batches)] if k == 2 else []
                add_sums(waiting)

        add_sums([(*chain, far) for chain in chains if top[chain] == far])
        if halved:
            add_sums([(*chain, far - 1) for chain in chains if top[chain] < far])
        total = {}
        for chain in chains:
            step = chain[1]
            if not halved:
                value = sums[(*chain, far)]
            else:
                value = next(sums[chain[0], way, far] for way in (1, -1) if top[chain[0], way] == far)[kept[step]]
            for place in range(far - 1, -1, -1):
                value = hop(value, -step)
                near = sums[(*chain, place)] if place else None
                if place and halved and place == far - 1:
                    fresh = added(value, near[kept[step]])
                    value = jnp.concatenate(
                        [fresh, near[part:]] if step == 1 else [near[: tok_rows - part], fresh]
                    )
                elif place:
                    value = added(value, near)
            total[chain] = value
        parts = [
            (arrived[b], sums[b, 1, 0], total[b, 1], total[b, -1]) for b in range(batches)
        ]
        return final_sums(parts)[None]

    return shards


def solution(mesh):
    placed = (
        P("section", None, "expert", None),
        P("section", None, "expert"),
        P("section", None, "expert", None),
        P("section", None, "expert", None),
        P("section", "expert", None, None),
        P("section", "expert", None, None),
        P("section", "expert", None, None),
        P("section", None, None),
    )
    return jax.shard_map(
        build(chip_cycle(mesh)),
        mesh=mesh,
        in_specs=placed,
        out_specs=P("section", None, "expert", None),
        check_vma=False,
    )
```
